256 devices in a mesh: grp: 16 (over z, core), head: 16 (over y, x).
Axes of the slice: x: 4, y: 4, z: 8, core: 2. Of those that a mesh axis runs over, the one named last changes fastest.
Arguments:
- queries: bfloat16 [32768, 4096], P(('grp', 'head')), may hold values from -10 to 10
- key_vectors: bfloat16 [32768, 1024], P(('grp', 'head')), may hold values from -10 to 10
- value_vectors: bfloat16 [32768, 1024], P(('grp', 'head')), may hold values from -6 to 6
- grad_out: bfloat16 [32768, 4096], P(('grp', 'head')), may hold values from -6 to 6
- doc_lengths: int32 [16, 3], replicated, may hold values from 1 to 1536, 2048 in all within a row
- parcel_shift: int32 [1], replicated, may hold values from 1 to 15
Outputs:
- attn_out: bfloat16 [32768, 4096], P(('grp', 'head'))
- grad_q: bfloat16 [32768, 4096], P(('grp', 'head'))
- grad_k: bfloat16 [32768, 1024], P(('grp', 'head'))
- grad_v: bfloat16 [32768, 1024], P(('grp', 'head'))
The draws below stay inside these ranges and needn't reach their ends.
Inputs may be any that keep to these rules, and one draw needn't show every extreme that they name: `doc_lengths`: each row holds the 3 document lengths of one parcel; they sum to 2048.
All inputs are finite; a program needn't handle non-finite values.
Results may differ from the reference program's by a relative error of at most 0.025.
Values may be sent and summed in bfloat16 or wider, within the bound.
No kernel may reach another device: no remote copies, remote signals or barrier semaphores. Data moves between devices by JAX's collectives and lax.ppermute only.
A program may use at most 64 MiB of HBM per device.

```python
import math
import jax
import jax.numpy as jnp
import numpy as np
from jax import lax

HEADS = 32
KV_HEADS = 8
HEAD_DIM = 128
DOCS = 3
COLS = 1
GROUPS = 16
PARCELS = 16
PARCEL = 2048
LONGEST = 1536
TOKENS = 32768


def draw_queries(key, part):
    key = jax.random.fold_in(key, 3)
    result = jnp.clip(jax.random.normal(key, (TOKENS, HEADS * HEAD_DIM), jnp.float32), -6.0, 6.0)
    return result.astype(jnp.bfloat16)


def draw_key_vectors(key, part):
    key = jax.random.fold_in(key, 5)
    result = jnp.clip(jax.random.normal(key, (TOKENS, KV_HEADS * HEAD_DIM), jnp.float32), -6.0, 6.0)
    return result.astype(jnp.bfloat16)


def level_of(rng, extent, pieces, smallest, largest):
    factor_of, own = 1.0, jax.random.fold_in(rng, 6)
    for position, parts in pieces:
        heights = jnp.exp(jax.random.uniform(jax.random.fold_in(own, position), (parts,), jnp.float32, smallest / len(pieces), largest / len(pieces)))
        factor_of = factor_of * jnp.repeat(heights, extent[position] // parts).reshape([-1 if axis == position else 1 for axis in range(len(extent))])
    return factor_of


def profile(count, total, bound, lean):
    portions = [(1 << 20) // math.isqrt(rank ** lean) + 1 for rank in range(2, count + 1)]
    surplus, holding = total - bound - (count - 1), [1] * (count - 1)
    while surplus > 0:
        movable = [i for i in range(count - 1) if holding[i] < bound]
        pool, budget = sum([portions[i] for i in movable]), surplus
        for i in movable:
            addition = min(bound - holding[i], max(1, budget * portions[i] // pool), surplus)
            holding[i] = holding[i] + addition
            surplus = surplus - addition
    return np.array([bound] + holding)


def ragged(rng, amount, total, most, skew):
    if amount == 2:
        one = jax.random.randint(rng, (), max(1, total - most), min(most, total - 1) + 1)
        return jnp.stack([one, total - one])
    lengths = jnp.asarray(profile(amount, total, most, skew), jnp.int32)
    twos = (amount - 1) // 2
    giver, receiver = lengths[1:1 + 2 * twos:2], lengths[2:2 + 2 * twos:2]
    room = jnp.minimum(giver - 1, most - receiver)
    moved = jax.random.randint(jax.random.fold_in(rng, 1), (twos,), 0, 1 << 20) % (room + 1)
    lengths = lengths.at[1:1 + 2 * twos:2].set(giver - moved).at[2:2 + 2 * twos:2].set(receiver + moved)
    return lengths[jax.random.permutation(jax.random.fold_in(rng, 2), amount)]


def bell_draw(rng, shape, width, most, cuts=(), kind=jnp.bfloat16):
    loudness = level_of(rng, shape, cuts, -0.22, 0.18) if cuts else 1.0
    array = jax.random.normal(rng, shape, jnp.float32) * width * loudness
    return jnp.minimum(jnp.maximum(array, -most), most).astype(kind)


def setup_inputs(seed: int = 0) -> dict:
    seeds = jax.random.split(jax.random.key(seed), 7)
    return {
        "queries": draw_queries(jax.random.fold_in(seeds[6], 71), 0),
        "key_vectors": draw_key_vectors(jax.random.fold_in(seeds[6], 71), 0),
        "value_vectors": bell_draw(seeds[2], (TOKENS, KV_HEADS * HEAD_DIM), 1.0, 6.0, ((0, 256),)),
        "grad_out": bell_draw(seeds[3], (TOKENS, HEADS * HEAD_DIM), 1.0, 6.0, ((0, 256),)),
        "doc_lengths": jax.vmap(lambda own: ragged(own, DOCS, PARCEL, LONGEST, 2))(jax.random.split(seeds[4], PARCELS)).reshape((PARCELS, DOCS)).astype(jnp.int32),
        "parcel_shift": jax.random.randint(seeds[5], (COLS,), 1, GROUPS).astype(jnp.int32),
    }


def parcel_attention(query_block, key_block, value_block, cotangent_block, doc_ids):
    parcel_len = doc_ids.shape[0]
    block_rows = math.gcd(parcel_len, 512)
    block_count = parcel_len // block_rows
    kv_count = key_block.shape[1]
    sharing = query_block.shape[2]
    feat = query_block.shape[3]
    scaling = feat ** -0.5
    positions = jnp.arange(parcel_len, dtype=jnp.int32)
    key_wide = key_block.astype(jnp.float32)
    value_wide = value_block.astype(jnp.float32)
    query_pieces = query_block.reshape(block_count, block_rows, kv_count, sharing, feat)
    cotangent_pieces = cotangent_block.reshape(block_count, block_rows, kv_count, sharing, feat)
    id_pieces = doc_ids.reshape(block_count, block_rows)
    starts = jnp.arange(block_count, dtype=jnp.int32) * block_rows

    def one_block(carry, operands):
        key_acc, value_acc = carry
        query_piece, cotangent_piece, id_piece, start = operands
        query_pos = start + jnp.arange(block_rows, dtype=jnp.int32)
        allowed = (id_piece[:, None] == doc_ids[None, :]) & (positions[None, :] <= query_pos[:, None])
        query_wide = query_piece.astype(jnp.float32)
        cotangent_wide = cotangent_piece.astype(jnp.float32)
        scores = jnp.einsum('qkgd,tkd->kgqt', query_wide, key_wide) * scaling
        scores = jnp.where(allowed, scores, -1e30)
        row_max = jnp.max(scores, axis=-1, keepdims=True)
        exponent = jnp.exp(scores - row_max)
        probs = exponent / jnp.sum(exponent, axis=-1, keepdims=True)
        weights = probs.astype(jnp.bfloat16)
        weights_wide = weights.astype(jnp.float32)
        output = jnp.einsum('kgqt,tkd->qkgd', weights_wide, value_wide).astype(jnp.bfloat16)
        row_delta = jnp.einsum('qkgd,qkgd->kgq', cotangent_wide, output.astype(jnp.float32))
        grad_prob = jnp.einsum('qkgd,tkd->kgqt', cotangent_wide, value_wide)
        grad_score = (probs * (grad_prob - row_delta[..., None])).astype(jnp.bfloat16)
        score_wide = grad_score.astype(jnp.float32)
        grad_query = (jnp.einsum('kgqt,tkd->qkgd', score_wide, key_wide) * scaling).astype(jnp.bfloat16)
        key_acc = key_acc + jnp.einsum('kgqt,qkgd->tkd', score_wide, query_wide) * scaling
        value_acc = value_acc + jnp.einsum('kgqt,qkgd->tkd', weights_wide, cotangent_wide)
        return (key_acc, value_acc), (output, grad_query)

    empty = jnp.zeros((parcel_len, kv_count, feat), jnp.float32)
    (grad_key, grad_value), (output, grad_query) = lax.scan(one_block, (empty, empty), (query_pieces, cotangent_pieces, id_pieces, starts))
    output = output.reshape(parcel_len, kv_count, sharing, feat)
    grad_query = grad_query.reshape(parcel_len, kv_count, sharing, feat)
    return output, grad_query, grad_key, grad_value


def attend_one(operands):
    return parcel_attention(operands[0], operands[1], operands[2], operands[3], operands[4])


def reference(queries, key_vectors, value_vectors, grad_out, doc_lengths, parcel_shift):
    row_ids = jnp.arange(GROUPS, dtype=jnp.int32)[:, None]
    col_ids = jnp.arange(COLS, dtype=jnp.int32)[None, :]
    source_of = (((row_ids - parcel_shift[None, :]) % GROUPS) * COLS + col_ids).reshape(-1).astype(jnp.int32)
    dest_of = (((row_ids + parcel_shift[None, :]) % GROUPS) * COLS + col_ids).reshape(-1).astype(jnp.int32)
    sharing = HEADS // KV_HEADS
    cotangent = jnp.take(grad_out.reshape(PARCELS, PARCEL, HEADS * HEAD_DIM), dest_of, axis=0)
    query_block = queries.reshape(PARCELS, PARCEL, KV_HEADS, sharing, HEAD_DIM)
    key_block = key_vectors.reshape(PARCELS, PARCEL, KV_HEADS, HEAD_DIM)
    value_block = value_vectors.reshape(PARCELS, PARCEL, KV_HEADS, HEAD_DIM)
    cotangent_block = cotangent.reshape(PARCELS, PARCEL, KV_HEADS, sharing, HEAD_DIM)
    doc_ends = jnp.cumsum(doc_lengths, axis=1)
    positions = jnp.arange(PARCEL, dtype=jnp.int32)
    doc_ids = jnp.sum((positions[None, :, None] >= doc_ends[:, None, :]).astype(jnp.int32), axis=2)
    output, grad_query, grad_key, grad_value = lax.map(attend_one, (query_block, key_block, value_block, cotangent_block, doc_ids))
    attn_out = jnp.take(output.reshape(PARCELS, PARCEL, HEADS * HEAD_DIM), source_of, axis=0).reshape(TOKENS, HEADS * HEAD_DIM)
    grad_q = grad_query.reshape(TOKENS, HEADS * HEAD_DIM)
    grad_k = grad_key.reshape(TOKENS, KV_HEADS * HEAD_DIM).astype(jnp.bfloat16)
    grad_v = grad_value.reshape(TOKENS, KV_HEADS * HEAD_DIM).astype(jnp.bfloat16)
    return (attn_out, grad_q, grad_k, grad_v)
```

```python
import functools
import math

import jax
import jax.numpy as jnp
from jax import lax
from jax.experimental import pallas as pl
from jax.experimental.pallas import tpu as pltpu
from jax.sharding import PartitionSpec as P

HEADS = 32
KV_HEADS = 8
FEAT = 128
BLOCK = 256
SCALING = FEAT**-0.5
LOG2_SCALING = SCALING * math.log2(math.e)
EXCLUDED = -1e30
NT = (((1,), (1,)), ((), ()))
NN = (((1,), (0,)), ((), ()))


def dot(a, b, dims=NN):
    return lax.dot_general(a, b, dims, preferred_element_type=jnp.float32)


def doc_ends(group_ref, lengths_ref):
    group = group_ref[0]
    first = lengths_ref[group, 0]
    return first, first + lengths_ref[group, 1]


def start_of(position, first, second):
    return jnp.where(position < first, 0, jnp.where(position < second, first, second))


def query_rows(block, heads, first, second):
    column = lax.broadcasted_iota(jnp.int32, (1, heads * BLOCK), 1)
    position = block * BLOCK + lax.rem(column, BLOCK)
    return position, start_of(position, first, second)


def masked_scores(keys, query, key_block, position, start):
    scores = dot(keys, query, NT) * LOG2_SCALING
    token = key_block * BLOCK + lax.broadcasted_iota(jnp.int32, (BLOCK, 1), 0)
    return jnp.where((token >= start) & (token <= position), scores, EXCLUDED)


def rows(block):
    return pl.ds(pl.multiple_of(block * BLOCK, BLOCK), BLOCK)


def stacked_heads(ref, block, heads):
    return jnp.concatenate(
        [ref[rows(block), h * FEAT : (h + 1) * FEAT] for h in range(heads)], axis=0
    )


def forward_kernel(heads, group_ref, lengths_ref, qkv_ref, out_ref, lse_ref, vt_ref):
    blocks = qkv_ref.shape[0] // BLOCK
    first, second = doc_ends(group_ref, lengths_ref)
    key_cols = slice(heads * FEAT, (heads + 1) * FEAT)
    value_cols = slice((heads + 1) * FEAT, (heads + 2) * FEAT)
    for block in range(blocks):
        vt_ref[block] = qkv_ref[block * BLOCK : (block + 1) * BLOCK, value_cols].T

    def one_query_block(block, _):
        query = stacked_heads(qkv_ref, block, heads)
        position, start = query_rows(block, heads, first, second)
        lowest = start_of(block * BLOCK, first, second) // BLOCK

        def one_key_block(key_block, carry):
            top, total, acc = carry
            scores = masked_scores(
                qkv_ref[rows(key_block), key_cols], query, key_block, position, start
            )
            new_top = jnp.maximum(top, jnp.max(scores, axis=0, keepdims=True))
            exponent = jnp.exp2(scores - new_top)
            shrink = jnp.exp2(top - new_top)
            total = total * shrink + jnp.sum(exponent, axis=0, keepdims=True)
            acc = acc * shrink + dot(vt_ref[key_block], exponent.astype(jnp.bfloat16))
            return new_top, total, acc

        columns = heads * BLOCK
        top, total, acc = lax.fori_loop(
            lowest,
            block + 1,
            one_key_block,
            (
                jnp.full((1, columns), EXCLUDED, jnp.float32),
                jnp.zeros((1, columns), jnp.float32),
                jnp.zeros((FEAT, columns), jnp.float32),
            ),
        )
        lse_ref[block] = top + jnp.log2(total)
        output = (acc / total).T.astype(jnp.bfloat16)
        for h in range(heads):
            out_ref[rows(block), h * FEAT : (h + 1) * FEAT] = output[h * BLOCK : (h + 1) * BLOCK]
        return 0

    lax.fori_loop(0, blocks, one_query_block, 0)


def backward_kernel(
    heads, group_ref, lengths_ref, qkv_ref, out_ref, cot_ref, lse_ref, grad_ref, kt_ref, dk_ref, dv_ref
):
    blocks = qkv_ref.shape[0] // BLOCK
    first, second = doc_ends(group_ref, lengths_ref)
    key_cols = slice(heads * FEAT, (heads + 1) * FEAT)
    value_cols = slice((heads + 1) * FEAT, (heads + 2) * FEAT)
    for block in range(blocks):
        kt_ref[block] = qkv_ref[block * BLOCK : (block + 1) * BLOCK, key_cols].T
    dk_ref[...] = jnp.zeros_like(dk_ref)
    dv_ref[...] = jnp.zeros_like(dv_ref)

    def one_query_block(block, _):
        query = stacked_heads(qkv_ref, block, heads)
        cotangent = stacked_heads(cot_ref, block, heads)
        output = stacked_heads(out_ref, block, heads)
        position, start = query_rows(block, heads, first, second)
        lowest = start_of(block * BLOCK, first, second) // BLOCK
        lse = lse_ref[block]
        product = cotangent.astype(jnp.float32) * output.astype(jnp.float32)
        delta = jnp.sum(product.T, axis=0, keepdims=True)

        def one_key_block(key_block, dq):
            here = rows(key_block)
            scores = masked_scores(
                qkv_ref[here, key_cols], query, key_block, position, start
            )
            probs = jnp.exp2(scores - lse)
            grad_prob = dot(qkv_ref[here, value_cols], cotangent, NT)
            grad_score = (probs * (grad_prob - delta)).astype(jnp.bfloat16)
            dv_ref[here, :] += dot(probs.astype(jnp.bfloat16), cotangent)
            dk_ref[here, :] += dot(grad_score, query)
            return dq + dot(kt_ref[key_block], grad_score)

        dq = lax.fori_loop(
            lowest, block + 1, one_key_block, jnp.zeros((FEAT, heads * BLOCK), jnp.float32)
        )
        dq = (dq * SCALING).T.astype(jnp.bfloat16)
        for h in range(heads):
            grad_ref[rows(block), h * FEAT : (h + 1) * FEAT] = dq[h * BLOCK : (h + 1) * BLOCK]
        return 0

    lax.fori_loop(0, blocks, one_query_block, 0)
    grad_ref[:, key_cols] = (dk_ref[...] * SCALING).astype(jnp.bfloat16)
    grad_ref[:, value_cols] = dv_ref[...].astype(jnp.bfloat16)


SMEM = pl.BlockSpec(memory_space=pltpu.SMEM)
VMEM = pl.BlockSpec(memory_space=pltpu.VMEM)
KERNEL_PARAMS = pltpu.CompilerParams(vmem_limit_bytes=40 * 2**20)


def attend(group, doc_lengths, qkv, heads):
    tokens = qkv.shape[0]
    blocks = tokens // BLOCK
    return pl.pallas_call(
        functools.partial(forward_kernel, heads),
        out_shape=(
            jax.ShapeDtypeStruct((tokens, heads * FEAT), jnp.bfloat16),
            jax.ShapeDtypeStruct((blocks, 1, heads * BLOCK), jnp.float32),
        ),
        in_specs=[SMEM, SMEM, VMEM],
        out_specs=(VMEM, VMEM),
        scratch_shapes=[pltpu.VMEM((blocks, FEAT, BLOCK), jnp.bfloat16)],
        compiler_params=KERNEL_PARAMS,
        cost_estimate=pl.CostEstimate(
            flops=2 * 2 * heads * tokens * tokens * FEAT,
            bytes_accessed=3 * 2**20,
            transcendentals=heads * tokens * tokens // 2,
        ),
    )(group, doc_lengths, qkv)


def attend_back(group, doc_lengths, qkv, output, cotangent, lse, heads):
    tokens = qkv.shape[0]
    blocks = tokens // BLOCK
    return pl.pallas_call(
        functools.partial(backward_kernel, heads),
        out_shape=jax.ShapeDtypeStruct(qkv.shape, jnp.bfloat16),
        in_specs=[SMEM, SMEM, VMEM, VMEM, VMEM, VMEM],
        out_specs=VMEM,
        scratch_shapes=[
            pltpu.VMEM((blocks, FEAT, BLOCK), jnp.bfloat16),
            pltpu.VMEM((tokens, FEAT), jnp.float32),
            pltpu.VMEM((tokens, FEAT), jnp.float32),
        ],
        compiler_params=KERNEL_PARAMS,
        cost_estimate=pl.CostEstimate(
            flops=5 * 2 * heads * tokens * tokens * FEAT,
            bytes_accessed=6 * 2**20,
            transcendentals=heads * tokens * tokens // 2,
        ),
    )(group, doc_lengths, qkv, output, cotangent, lse)


def over_heads(block):
    return lax.all_to_all(block, "head", split_axis=0, concat_axis=0, tiled=True)


def along_rows(block, distance):
    count = lax.axis_size("grp")
    return lax.ppermute(block, "grp", [(i, (i + distance) % count) for i in range(count)])


def by_device(block, devices):
    return block.reshape(block.shape[0], devices, -1).swapaxes(0, 1)


def by_token(block):
    return block.swapaxes(0, 1).reshape(block.shape[1], -1)


def one_shift(shift, late, queries, key_vectors, value_vectors, grad_out, doc_lengths, group):
    devices = lax.axis_size("head")
    tokens = queries.shape[0]
    heads = HEADS // devices
    repeats = devices // KV_HEADS

    def widened(block):
        block = block.reshape(tokens, KV_HEADS, 1, FEAT).transpose(1, 2, 0, 3)
        block = jnp.broadcast_to(block, (KV_HEADS, repeats, tokens, FEAT))
        return block.reshape(devices, tokens, FEAT)

    cotangent = along_rows(grad_out, -shift)
    qkv = jnp.concatenate(
        [by_device(queries, devices), widened(key_vectors), widened(value_vectors)], axis=2
    )
    qkv = over_heads(qkv).reshape(devices * tokens, -1)
    output, lse = attend(group, doc_lengths, qkv, heads)
    shaped = output.reshape(devices, tokens, -1)
    cotangent = by_device(cotangent, devices)
    if late:
        attn = over_heads(shaped)
        cotangent, attn = lax.optimization_barrier((cotangent, attn))
        cotangent = over_heads(cotangent)
    else:
        cotangent = over_heads(cotangent)
        shaped, cotangent = lax.optimization_barrier((shaped, cotangent))
        attn = over_heads(shaped)
    attn_out = along_rows(by_token(attn), shift)
    cotangent = cotangent.reshape(devices * tokens, -1)
    grads = attend_back(group, doc_lengths, qkv, output, cotangent, lse, heads)
    grads = grads.reshape(devices, tokens, -1)
    grads, _ = lax.optimization_barrier((grads, attn))
    grads = over_heads(grads)
    grad_q = by_token(grads[:, :, : heads * FEAT])

    def summed(block):
        block = block.reshape(KV_HEADS, repeats, tokens, FEAT).astype(jnp.float32).sum(axis=1)
        return by_token(block.astype(jnp.bfloat16))

    grad_k = summed(grads[:, :, heads * FEAT : (heads + 1) * FEAT])
    grad_v = summed(grads[:, :, (heads + 1) * FEAT :])
    return attn_out, grad_q, grad_k, grad_v


def shards(queries, key_vectors, value_vectors, grad_out, doc_lengths, parcel_shift):
    rows_count = lax.axis_size("grp")
    group = lax.axis_index("grp").astype(jnp.int32).reshape(1)
    branches = [
        functools.partial(one_shift, shift, min(shift, rows_count - shift) > 3)
        for shift in range(1, rows_count)
    ]
    return lax.switch(
        parcel_shift[0] - 1,
        branches,
        queries,
        key_vectors,
        value_vectors,
        grad_out,
        doc_lengths,
        group,
    )


def solution(mesh):
    split = P(("grp", "head"), None)
    return jax.shard_map(
        shards,
        mesh=mesh,
        in_specs=(split, split, split, split, P(), P()),
        out_specs=(split, split, split, split),
        check_vma=False,
    )
```

```python
import functools
import math

import jax
import jax.numpy as jnp
from jax import lax
from jax.experimental import pallas as pl
from jax.experimental.pallas import tpu as pltpu
from jax.sharding import PartitionSpec as P

HEADS = 32
KV_HEADS = 8
FEAT = 128
DOCS = 3
BLOCK = 512
SCALING = FEAT**-0.5
LOG2_SCALING = SCALING * math.log2(math.e)
EXCLUDED = -1e30


def dot(a, b):
    return jnp.dot(a, b, preferred_element_type=jnp.float32)


def rows(block):
    return pl.ds(pl.multiple_of(block * BLOCK, BLOCK), BLOCK)


def start_of(position, first, second):
    return jnp.where(position < first, 0, jnp.where(position < second, first, second))


def lanes_and_documents(block, first, second):
    lane = lax.broadcasted_iota(jnp.int32, (BLOCK, FEAT), 1)
    position = block * BLOCK + lax.broadcasted_iota(jnp.int32, (BLOCK, FEAT), 0)
    return lane, (position >= first).astype(jnp.int32) + (position >= second).astype(jnp.int32)


def in_lanes(lane, column):
    high = column.astype(jnp.bfloat16).astype(jnp.float32)
    middle = (column - high).astype(jnp.bfloat16).astype(jnp.float32)
    low = column - high - middle
    picked = jnp.where(lane == DOCS, high, jnp.where(lane == DOCS + 1, middle, low))
    return jnp.where((lane >= DOCS) & (lane < DOCS + 3), picked, 0.0)


def fill_key_marks(marks_ref, block, first, second):
    lane, document = lanes_and_documents(block, first, second)
    marked = (lane == document) | ((lane >= DOCS) & (lane < DOCS + 3))
    marks_ref[rows(block), :] = marked.astype(jnp.float32).astype(jnp.bfloat16)


def causal(values, other):
    key = lax.broadcasted_iota(jnp.int32, values.shape, 0)
    query = lax.rem(lax.broadcasted_iota(jnp.int32, values.shape, 1), BLOCK)
    return jnp.where(key <= query, values, other)


def causal_rows(values):
    query = lax.rem(lax.broadcasted_iota(jnp.int32, values.shape, 0), BLOCK)
    key = lax.broadcasted_iota(jnp.int32, values.shape, 1)
    return jnp.where(key <= query, values, EXCLUDED)


def folded(combine, values):
    parts = [values[:, at : at + FEAT] for at in range(0, values.shape[1], FEAT)]
    return functools.reduce(combine, parts)


def forward_kernel(
    heads,
    group_ref,
    lengths_ref,
    qkv_ref,
    out_ref,
    marks_ref,
    kt_ref,
    query_ref,
    scores_ref,
    top_ref,
    total_ref,
    acc_ref,
):
    blocks = qkv_ref.shape[0] // BLOCK
    group = group_ref[0]
    first = lengths_ref[group, 0]
    second = first + lengths_ref[group, 1]
    key_cols = slice(heads * FEAT, (heads + 1) * FEAT)
    value_cols = slice((heads + 1) * FEAT, (heads + 2) * FEAT)

    def prepare(block, _):
        kt_ref[block, :FEAT, :] = qkv_ref[rows(block), key_cols].T
        kind = lax.broadcasted_iota(jnp.int32, (FEAT, BLOCK), 0)
        position = block * BLOCK + lax.broadcasted_iota(jnp.int32, (FEAT, BLOCK), 1)
        document = (position >= first).astype(jnp.int32) + (position >= second).astype(jnp.int32)
        kt_ref[block, FEAT:, :] = (kind == document).astype(jnp.float32).astype(jnp.bfloat16)
        return 0

    lax.fori_loop(0, blocks, prepare, 0)

    def one_query_block(block, _):
        lane, document = lanes_and_documents(block, first, second)
        marks = jnp.where((lane != document) & (lane < DOCS), EXCLUDED, 0.0)
        for h in range(heads):
            query_ref[h * BLOCK : (h + 1) * BLOCK, :FEAT] = qkv_ref[
                rows(block), h * FEAT : (h + 1) * FEAT
            ]
            query_ref[h * BLOCK : (h + 1) * BLOCK, FEAT:] = marks.astype(jnp.bfloat16)
        lowest = start_of(block * BLOCK, first, second) // BLOCK
        scores = causal_rows(dot(query_ref[...], kt_ref[block]))
        scores_ref[block] = scores
        top_ref[...] = folded(jnp.maximum, scores)

        def earlier(key_block, _):
            scores = dot(query_ref[...], kt_ref[key_block])
            scores_ref[key_block] = scores
            top_ref[...] = jnp.maximum(top_ref[...], folded(jnp.maximum, scores))
            return 0

        lax.fori_loop(lowest, block, earlier, 0)
        top = jnp.max(top_ref[...], axis=1, keepdims=True) * LOG2_SCALING
        top_ref[...] = jnp.broadcast_to(top, top_ref.shape)
        total_ref[...] = jnp.zeros_like(total_ref)
        acc_ref[...] = jnp.zeros_like(acc_ref)

        def weigh(key_block, _):
            top = top_ref[...]
            exponent = jnp.exp2(
                scores_ref[key_block] * LOG2_SCALING - jnp.concatenate([top] * (BLOCK // FEAT), axis=1)
            )
            total_ref[...] += folded(jnp.add, exponent)
            acc_ref[...] += dot(exponent.astype(jnp.bfloat16), qkv_ref[rows(key_block), value_cols])
            return 0

        lax.fori_loop(lowest, block + 1, weigh, 0)
        total = jnp.sum(total_ref[...], axis=1, keepdims=True)
        output = (acc_ref[...] * (1.0 / total)).astype(jnp.bfloat16)
        lse = (top + jnp.log2(total)) * (-1.0 / LOG2_SCALING)
        for h in range(heads):
            here = slice(h * BLOCK, (h + 1) * BLOCK)
            out_ref[rows(block), h * FEAT : (h + 1) * FEAT] = output[here]
            marks_ref[rows(block), h * FEAT : (h + 1) * FEAT] = (
                marks + in_lanes(lane, lse[here])
            ).astype(jnp.bfloat16)
        return 0

    lax.fori_loop(0, blocks, one_query_block, 0)


def backward_kernel(
    heads,
    group_ref,
    lengths_ref,
    qkv_ref,
    out_ref,
    marks_ref,
    cot_ref,
    grad_ref,
    key_marks_ref,
    kt_ref,
    query_ref,
    cotangent_ref,
    query_t_ref,
    cotangent_t_ref,
    dq_ref,
    dk_ref,
    dv_ref,
):
    blocks = qkv_ref.shape[0] // BLOCK
    group = group_ref[0]
    first = lengths_ref[group, 0]
    second = first + lengths_ref[group, 1]
    key_cols = slice(heads * FEAT, (heads + 1) * FEAT)
    value_cols = slice((heads + 1) * FEAT, (heads + 2) * FEAT)

    def prepare(block, _):
        fill_key_marks(key_marks_ref, block, first, second)
        kt_ref[block] = qkv_ref[rows(block), key_cols].T
        dk_ref[rows(block), :] = jnp.zeros((BLOCK, FEAT), jnp.float32)
        dv_ref[rows(block), :] = jnp.zeros((BLOCK, FEAT), jnp.float32)
        return 0

    lax.fori_loop(0, blocks, prepare, 0)

    def one_query_block(block, _):
        lane = lax.broadcasted_iota(jnp.int32, (BLOCK, FEAT), 1)
        for h in range(heads):
            here = slice(h * BLOCK, (h + 1) * BLOCK)
            cols = slice(h * FEAT, (h + 1) * FEAT)
            query_ref[here, :FEAT] = qkv_ref[rows(block), cols]
            query_ref[here, FEAT:] = marks_ref[rows(block), cols]
            cotangent = cot_ref[rows(block), cols]
            product = cotangent.astype(jnp.float32) * out_ref[rows(block), cols].astype(jnp.float32)
            delta = jnp.sum(product, axis=1, keepdims=True)
            cotangent_ref[here, :FEAT] = cotangent
            cotangent_ref[here, FEAT:] = in_lanes(lane, -delta).astype(jnp.bfloat16)
        query_t_ref[...] = query_ref[...].T
        cotangent_t_ref[...] = cotangent_ref[...].T
        lowest = start_of(block * BLOCK, first, second) // BLOCK
        dq_ref[...] = jnp.zeros_like(dq_ref)

        def one_key_block(key_block, diagonal):
            here = rows(key_block)
            key_marks = key_marks_ref[here, :]
            keys = jnp.concatenate([qkv_ref[here, key_cols], key_marks], axis=1)
            values = jnp.concatenate([qkv_ref[here, value_cols], key_marks], axis=1)
            probs = jnp.exp2(dot(keys, query_t_ref[...]) * LOG2_SCALING)
            if diagonal:
                probs = causal(probs, 0.0)
            grad_score = probs * dot(values, cotangent_t_ref[...])
            grad_score = grad_score.astype(jnp.bfloat16)
            dv_ref[here, :] += dot(probs.astype(jnp.bfloat16), cotangent_ref[:, :FEAT])
            dk_ref[here, :] += dot(grad_score, query_ref[:, :FEAT])
            dq_ref[...] += dot(kt_ref[key_block], grad_score)

        def earlier(key_block, _):
            one_key_block(key_block, False)
            return 0

        lax.fori_loop(lowest, block, earlier, 0)
        one_key_block(block, True)
        dq = (dq_ref[...] * SCALING).T.astype(jnp.bfloat16)
        for h in range(heads):
            grad_ref[rows(block), h * FEAT : (h + 1) * FEAT] = dq[h * BLOCK : (h + 1) * BLOCK]
        return 0

    lax.fori_loop(0, blocks, one_query_block, 0)

    def finish(block, _):
        grad_ref[rows(block), key_cols] = (dk_ref[rows(block), :] * SCALING).astype(jnp.bfloat16)
        grad_ref[rows(block), value_cols] = dv_ref[rows(block), :].astype(jnp.bfloat16)
        return 0

    lax.fori_loop(0, blocks, finish, 0)


SMEM = pl.BlockSpec(memory_space=pltpu.SMEM)
VMEM = pl.BlockSpec(memory_space=pltpu.VMEM)
KERNEL_PARAMS = pltpu.CompilerParams(vmem_limit_bytes=40 * 2**20)


def attend(group, doc_lengths, qkv, heads):
    tokens = qkv.shape[0]
    blocks = tokens // BLOCK
    columns = heads * BLOCK
    wide = jax.ShapeDtypeStruct((tokens, heads * FEAT), jnp.bfloat16)
    return pl.pallas_call(
        functools.partial(forward_kernel, heads),
        out_shape=(wide, wide),
        in_specs=[SMEM, SMEM, VMEM],
        out_specs=(VMEM, VMEM),
        scratch_shapes=[
            pltpu.VMEM((blocks, 2 * FEAT, BLOCK), jnp.bfloat16),
            pltpu.VMEM((columns, 2 * FEAT), jnp.bfloat16),
            pltpu.VMEM((blocks, columns, BLOCK), jnp.float32),
            pltpu.VMEM((columns, FEAT), jnp.float32),
            pltpu.VMEM((columns, FEAT), jnp.float32),
            pltpu.VMEM((columns, FEAT), jnp.float32),
        ],
        compiler_params=KERNEL_PARAMS,
        cost_estimate=pl.CostEstimate(
            flops=2 * 2 * heads * tokens * tokens * FEAT,
            bytes_accessed=4 * 2**20,
            transcendentals=heads * tokens * tokens // 2,
        ),
    )(group, doc_lengths, qkv)


def attend_back(group, doc_lengths, qkv, output, marks, cotangent, heads):
    tokens = qkv.shape[0]
    blocks = tokens // BLOCK
    columns = heads * BLOCK
    return pl.pallas_call(
        functools.partial(backward_kernel, heads),
        out_shape=jax.ShapeDtypeStruct(qkv.shape, jnp.bfloat16),
        in_specs=[SMEM, SMEM, VMEM, VMEM, VMEM, VMEM],
        out_specs=VMEM,
        scratch_shapes=[
            pltpu.VMEM((tokens, FEAT), jnp.bfloat16),
            pltpu.VMEM((blocks, FEAT, BLOCK), jnp.bfloat16),
            pltpu.VMEM((columns, 2 * FEAT), jnp.bfloat16),
            pltpu.VMEM((columns, 2 * FEAT), jnp.bfloat16),
            pltpu.VMEM((2 * FEAT, columns), jnp.bfloat16),
            pltpu.VMEM((2 * FEAT, columns), jnp.bfloat16),
            pltpu.VMEM((FEAT, columns), jnp.float32),
            pltpu.VMEM((tokens, FEAT), jnp.float32),
            pltpu.VMEM((tokens, FEAT), jnp.float32),
        ],
        compiler_params=KERNEL_PARAMS,
        cost_estimate=pl.CostEstimate(
            flops=5 * 2 * heads * tokens * tokens * FEAT,
            bytes_accessed=7 * 2**20,
            transcendentals=heads * tokens * tokens // 2,
        ),
    )(group, doc_lengths, qkv, output, marks, cotangent)


def prologue_kernel(repeats, q_ref, k_ref, v_ref, cot_ref, qkv_ref, cot_by_device_ref):
    devices, _, width = cot_by_device_ref.shape
    for device in range(devices):
        cols = slice(device * width, (device + 1) * width)
        shared = slice(device // repeats * FEAT, (device // repeats + 1) * FEAT)
        qkv_ref[device, :, :width] = q_ref[:, cols]
        qkv_ref[device, :, width : width + FEAT] = k_ref[:, shared]
        qkv_ref[device, :, width + FEAT :] = v_ref[:, shared]
        cot_by_device_ref[device] = cot_ref[:, cols]


def by_device(queries, key_vectors, value_vectors, grad_out, devices):
    tokens = queries.shape[0]
    width = queries.shape[1] // devices
    return pl.pallas_call(
        functools.partial(prologue_kernel, devices // KV_HEADS),
        out_shape=(
            jax.ShapeDtypeStruct((devices, tokens, width + 2 * FEAT), jnp.bfloat16),
            jax.ShapeDtypeStruct((devices, tokens, width), jnp.bfloat16),
        ),
        in_specs=[VMEM] * 4,
        out_specs=(VMEM, VMEM),
        compiler_params=KERNEL_PARAMS,
    )(queries, key_vectors, value_vectors, grad_out)


def epilogue_kernel(repeats, grads_ref, attn_ref, out_ref, dq_ref, dk_ref, dv_ref):
    devices, _, width = attn_ref.shape
    for device in range(devices):
        cols = slice(device * width, (device + 1) * width)
        out_ref[:, cols] = attn_ref[device]
        dq_ref[:, cols] = grads_ref[device, :, :width]
    for head in range(devices // repeats):
        cols = slice(head * FEAT, (head + 1) * FEAT)
        for ref, at in ((dk_ref, width), (dv_ref, width + FEAT)):
            parts = [
                grads_ref[head * repeats + part, :, at : at + FEAT].astype(jnp.float32)
                for part in range(repeats)
            ]
            ref[:, cols] = functools.reduce(jnp.add, parts).astype(jnp.bfloat16)


def by_token(grads, attn):
    devices, tokens, width = attn.shape
    wide = jax.ShapeDtypeStruct((tokens, devices * width), jnp.bfloat16)
    narrow = jax.ShapeDtypeStruct((tokens, KV_HEADS * FEAT), jnp.bfloat16)
    return pl.pallas_call(
        functools.partial(epilogue_kernel, devices // KV_HEADS),
        out_shape=(wide, wide, narrow, narrow),
        in_specs=[VMEM] * 2,
        out_specs=(VMEM,) * 4,
        compiler_params=KERNEL_PARAMS,
    )(grads, attn)


def over_heads(block):
    return lax.all_to_all(block, "head", split_axis=0, concat_axis=0, tiled=True)


def along_rows(block, distance):
    count = lax.axis_size("grp")
    return lax.ppermute(block, "grp", [(i, (i + distance) % count) for i in range(count)])


def first_part(shift, qkv, cotangent):
    return over_heads(qkv), along_rows(cotangent, -shift)


def last_part(shift, grads, attn):
    return over_heads(grads), along_rows(attn, shift)


def shards(queries, key_vectors, value_vectors, grad_out, doc_lengths, parcel_shift):
    group = lax.axis_index("grp").astype(jnp.int32).reshape(1)
    devices = lax.axis_size("head")
    heads = HEADS // devices
    shifts = range(1, lax.axis_size("grp"))
    choice = parcel_shift[0] - 1

    qkv, cotangent = by_device(queries, key_vectors, value_vectors, grad_out, devices)
    shape = cotangent.shape
    qkv, cotangent = lax.switch(
        choice, [functools.partial(first_part, s) for s in shifts], qkv, cotangent
    )
    qkv = qkv.reshape(shape[0] * shape[1], -1)
    cotangent = over_heads(cotangent)
    output, marks = attend(group, doc_lengths, qkv, heads)
    attn, cotangent = lax.optimization_barrier((output.reshape(shape), cotangent))
    attn = over_heads(attn)
    cotangent = cotangent.reshape(output.shape)
    grads = attend_back(group, doc_lengths, qkv, output, marks, cotangent, heads)
    grads = grads.reshape(shape[0], shape[1], -1)
    grads, attn = lax.switch(
        choice, [functools.partial(last_part, s) for s in shifts], grads, attn
    )
    return by_token(grads, attn)


def solution(mesh):
    split = P(("grp", "head"), None)
    return jax.shard_map(
        shards,
        mesh=mesh,
        in_specs=(split, split, split, split, P(), P()),
        out_specs=(split, split, split, split),
        check_vma=False,
    )
```

```python
import functools
import math

import jax
import jax.numpy as jnp
from jax import lax
from jax.experimental import pallas as pl
from jax.experimental.pallas import tpu as pltpu
from jax.sharding import PartitionSpec as P

HEADS = 32
KV_HEADS = 8
FEAT = 128
DOCS = 3
BLOCK = 512
SCALING = FEAT**-0.5
LOG2_SCALING = SCALING * math.log2(math.e)
EXCLUDED = -1e30


def dot(a, b):
    return jnp.dot(a, b, preferred_element_type=jnp.float32)


def rows(block):
    return pl.ds(pl.multiple_of(block * BLOCK, BLOCK), BLOCK)


def start_of(position, first, second):
    return jnp.where(position < first, 0, jnp.where(position < second, first, second))


def lanes_and_documents(block, first, second):
    lane = lax.broadcasted_iota(jnp.int32, (BLOCK, FEAT), 1)
    position = block * BLOCK + lax.broadcasted_iota(jnp.int32, (BLOCK, FEAT), 0)
    return lane, (position >= first).astype(jnp.int32) + (position >= second).astype(jnp.int32)


def in_lanes(lane, column):
    high = column.astype(jnp.bfloat16).astype(jnp.float32)
    middle = (column - high).astype(jnp.bfloat16).astype(jnp.float32)
    low = column - high - middle
    picked = jnp.where(lane == DOCS, high, jnp.where(lane == DOCS + 1, middle, low))
    return jnp.where((lane >= DOCS) & (lane < DOCS + 3), picked, 0.0)


def fill_key_marks(marks_ref, block, first, second):
    lane, document = lanes_and_documents(block, first, second)
    marked = (lane == document) | ((lane >= DOCS) & (lane < DOCS + 3))
    marks_ref[rows(block), :] = marked.astype(jnp.float32).astype(jnp.bfloat16)


def causal(values, other):
    key = lax.broadcasted_iota(jnp.int32, values.shape, 0)
    query = lax.rem(lax.broadcasted_iota(jnp.int32, values.shape, 1), BLOCK)
    return jnp.where(key <= query, values, other)


def causal_rows(values):
    query = lax.rem(lax.broadcasted_iota(jnp.int32, values.shape, 0), BLOCK)
    key = lax.broadcasted_iota(jnp.int32, values.shape, 1)
    return jnp.where(key <= query, values, EXCLUDED)


def folded(combine, values):
    parts = [values[:, at : at + FEAT] for at in range(0, values.shape[1], FEAT)]
    return functools.reduce(combine, parts)


def forward_kernel(
    heads,
    group_ref,
    lengths_ref,
    qkv_hbm,
    out_hbm,
    marks_hbm,
    qkv_ref,
    out_ref,
    marks_ref,
    kt_ref,
    query_ref,
    scores_ref,
    top_ref,
    total_ref,
    acc_ref,
    in_sems,
    out_sems,
):
    blocks = qkv_ref.shape[0] // BLOCK
    group = group_ref[0]
    first = lengths_ref[group, 0]
    second = first + lengths_ref[group, 1]
    key_cols = slice(heads * FEAT, (heads + 1) * FEAT)
    value_cols = slice((heads + 1) * FEAT, (heads + 2) * FEAT)

    def arrival(block):
        here = rows(block)
        return pltpu.make_async_copy(qkv_hbm.at[here, :], qkv_ref.at[here, :], in_sems.at[block])

    def departures(block):
        here = rows(block)
        return (
            pltpu.make_async_copy(out_ref.at[here, :], out_hbm.at[here, :], out_sems.at[0, block]),
            pltpu.make_async_copy(
                marks_ref.at[here, :], marks_hbm.at[here, :], out_sems.at[1, block]
            ),
        )

    for block in range(blocks):
        arrival(block).start()

    def one_query_block(block, _):
        arrival(block).wait()
        kt_ref[block, :FEAT, :] = qkv_ref[rows(block), key_cols].T
        kind = lax.broadcasted_iota(jnp.int32, (FEAT, BLOCK), 0)
        position = block * BLOCK + lax.broadcasted_iota(jnp.int32, (FEAT, BLOCK), 1)
        document = (position >= first).astype(jnp.int32) + (position >= second).astype(jnp.int32)
        kt_ref[block, FEAT:, :] = (kind == document).astype(jnp.float32).astype(jnp.bfloat16)
        lane, document = lanes_and_documents(block, first, second)
        marks = jnp.where((lane != document) & (lane < DOCS), EXCLUDED, 0.0)
        for h in range(heads):
            query_ref[h * BLOCK : (h + 1) * BLOCK, :FEAT] = qkv_ref[
                rows(block), h * FEAT : (h + 1) * FEAT
            ]
            query_ref[h * BLOCK : (h + 1) * BLOCK, FEAT:] = marks.astype(jnp.bfloat16)
        lowest = start_of(block * BLOCK, first, second) // BLOCK
        scores = causal_rows(dot(query_ref[...], kt_ref[block]))
        scores_ref[block] = scores
        top_ref[...] = folded(jnp.maximum, scores)

        def earlier(key_block, _):
            scores = dot(query_ref[...], kt_ref[key_block])
            scores_ref[key_block] = scores
            top_ref[...] = jnp.maximum(top_ref[...], folded(jnp.maximum, scores))
            return 0

        lax.fori_loop(lowest, block, earlier, 0)
        top = jnp.max(top_ref[...], axis=1, keepdims=True) * LOG2_SCALING
        top_ref[...] = jnp.broadcast_to(top, top_ref.shape)
        total_ref[...] = jnp.zeros_like(total_ref)
        acc_ref[...] = jnp.zeros_like(acc_ref)

        def weigh(key_block, _):
            top = top_ref[...]
            exponent = jnp.exp2(
                scores_ref[key_block] * LOG2_SCALING - jnp.concatenate([top] * (BLOCK // FEAT), axis=1)
            )
            total_ref[...] += folded(jnp.add, exponent)
            acc_ref[...] += dot(exponent.astype(jnp.bfloat16), qkv_ref[rows(key_block), value_cols])
            return 0

        lax.fori_loop(lowest, block + 1, weigh, 0)
        total = jnp.sum(total_ref[...], axis=1, keepdims=True)
        output = (acc_ref[...] * (1.0 / total)).astype(jnp.bfloat16)
        lse = (top + jnp.log2(total)) * (-1.0 / LOG2_SCALING)
        for h in range(heads):
            here = slice(h * BLOCK, (h + 1) * BLOCK)
            out_ref[rows(block), h * FEAT : (h + 1) * FEAT] = output[here]
            marks_ref[rows(block), h * FEAT : (h + 1) * FEAT] = (
                marks + in_lanes(lane, lse[here])
            ).astype(jnp.bfloat16)
        for departure in departures(block):
            departure.start()
        return 0

    lax.fori_loop(0, blocks, one_query_block, 0)
    for block in range(blocks):
        for departure in departures(block):
            departure.wait()


def backward_kernel(
    heads,
    group_ref,
    lengths_ref,
    qkv_hbm,
    out_hbm,
    marks_hbm,
    cot_hbm,
    grad_hbm,
    qkv_ref,
    out_ref,
    marks_ref,
    cot_ref,
    grad_ref,
    key_marks_ref,
    kt_ref,
    query_ref,
    cotangent_ref,
    query_t_ref,
    cotangent_t_ref,
    dq_ref,
    dk_ref,
    dv_ref,
    in_sems,
    out_sems,
):
    blocks = qkv_ref.shape[0] // BLOCK
    group = group_ref[0]
    first = lengths_ref[group, 0]
    second = first + lengths_ref[group, 1]
    query_cols = slice(0, heads * FEAT)
    key_cols = slice(heads * FEAT, (heads + 1) * FEAT)
    value_cols = slice((heads + 1) * FEAT, (heads + 2) * FEAT)
    shared_cols = slice(heads * FEAT, (heads + 2) * FEAT)

    def arrivals(block):
        here = rows(block)
        pairs = ((qkv_hbm, qkv_ref), (out_hbm, out_ref), (marks_hbm, marks_ref), (cot_hbm, cot_ref))
        return [
            pltpu.make_async_copy(source.at[here, :], target.at[here, :], in_sems.at[n, block])
            for n, (source, target) in enumerate(pairs)
        ]

    def departure(block, cols, which):
        here = rows(block)
        return pltpu.make_async_copy(
            grad_ref.at[here, cols], grad_hbm.at[here, cols], out_sems.at[which, block]
        )

    for block in range(blocks):
        for arrival in arrivals(block):
            arrival.start()

    def one_query_block(block, _):
        for arrival in arrivals(block):
            arrival.wait()
        fill_key_marks(key_marks_ref, block, first, second)
        kt_ref[block] = qkv_ref[rows(block), key_cols].T
        dk_ref[rows(block), :] = jnp.zeros((BLOCK, FEAT), jnp.float32)
        dv_ref[rows(block), :] = jnp.zeros((BLOCK, FEAT), jnp.float32)
        lane = lax.broadcasted_iota(jnp.int32, (BLOCK, FEAT), 1)
        for h in range(heads):
            here = slice(h * BLOCK, (h + 1) * BLOCK)
            cols = slice(h * FEAT, (h + 1) * FEAT)
            query_ref[here, :FEAT] = qkv_ref[rows(block), cols]
            query_ref[here, FEAT:] = marks_ref[rows(block), cols]
            cotangent = cot_ref[rows(block), cols]
            product = cotangent.astype(jnp.float32) * out_ref[rows(block), cols].astype(jnp.float32)
            delta = jnp.sum(product, axis=1, keepdims=True)
            cotangent_ref[here, :FEAT] = cotangent
            cotangent_ref[here, FEAT:] = in_lanes(lane, -delta).astype(jnp.bfloat16)
        query_t_ref[...] = query_ref[...].T
        cotangent_t_ref[...] = cotangent_ref[...].T
        lowest = start_of(block * BLOCK, first, second) // BLOCK
        dq_ref[...] = jnp.zeros_like(dq_ref)

        def one_key_block(key_block, diagonal):
            here = rows(key_block)
            key_marks = key_marks_ref[here, :]
            keys = jnp.concatenate([qkv_ref[here, key_cols], key_marks], axis=1)
            values = jnp.concatenate([qkv_ref[here, value_cols], key_marks], axis=1)
            probs = jnp.exp2(dot(keys, query_t_ref[...]) * LOG2_SCALING)
            if diagonal:
                probs = causal(probs, 0.0)
            grad_score = probs * dot(values, cotangent_t_ref[...])
            grad_score = grad_score.astype(jnp.bfloat16)
            dv_ref[here, :] += dot(probs.astype(jnp.bfloat16), cotangent_ref[:, :FEAT])
            dk_ref[here, :] += dot(grad_score, query_ref[:, :FEAT])
            dq_ref[...] += dot(kt_ref[key_block], grad_score)

        def earlier(key_block, _):
            one_key_block(key_block, False)
            return 0

        lax.fori_loop(lowest, block, earlier, 0)
        one_key_block(block, True)
        dq = (dq_ref[...] * SCALING).T.astype(jnp.bfloat16)
        for h in range(heads):
            grad_ref[rows(block), h * FEAT : (h + 1) * FEAT] = dq[h * BLOCK : (h + 1) * BLOCK]
        departure(block, query_cols, 0).start()
        return 0

    lax.fori_loop(0, blocks, one_query_block, 0)

    def finish(block, _):
        grad_ref[rows(block), key_cols] = (dk_ref[rows(block), :] * SCALING).astype(jnp.bfloat16)
        grad_ref[rows(block), value_cols] = dv_ref[rows(block), :].astype(jnp.bfloat16)
        departure(block, shared_cols, 1).start()
        return 0

    lax.fori_loop(0, blocks, finish, 0)
    for block in range(blocks):
        departure(block, query_cols, 0).wait()
        departure(block, shared_cols, 1).wait()


SMEM = pl.BlockSpec(memory_space=pltpu.SMEM)
VMEM = pl.BlockSpec(memory_space=pltpu.VMEM)
ANY = pl.BlockSpec(memory_space=pl.ANY)
SMALL = pltpu.CompilerParams(vmem_limit_bytes=32 * 2**20)
LARGE = pltpu.CompilerParams(vmem_limit_bytes=56 * 2**20)


def attend(group, doc_lengths, qkv, heads):
    tokens = qkv.shape[0]
    blocks = tokens // BLOCK
    columns = heads * BLOCK
    wide = jax.ShapeDtypeStruct((tokens, heads * FEAT), jnp.bfloat16)
    return pl.pallas_call(
        functools.partial(forward_kernel, heads),
        out_shape=(wide, wide),
        in_specs=[SMEM, SMEM, ANY],
        out_specs=(ANY, ANY),
        scratch_shapes=[
            pltpu.VMEM(qkv.shape, jnp.bfloat16),
            pltpu.VMEM(wide.shape, jnp.bfloat16),
            pltpu.VMEM(wide.shape, jnp.bfloat16),
            pltpu.VMEM((blocks, 2 * FEAT, BLOCK), jnp.bfloat16),
            pltpu.VMEM((columns, 2 * FEAT), jnp.bfloat16),
            pltpu.VMEM((blocks, columns, BLOCK), jnp.float32),
            pltpu.VMEM((columns, FEAT), jnp.float32),
            pltpu.VMEM((columns, FEAT), jnp.float32),
            pltpu.VMEM((columns, FEAT), jnp.float32),
            pltpu.SemaphoreType.DMA((blocks,)),
            pltpu.SemaphoreType.DMA((2, blocks)),
        ],
        compiler_params=LARGE,
        cost_estimate=pl.CostEstimate(
            flops=2 * 2 * heads * tokens * tokens * FEAT,
            bytes_accessed=4 * 2**20,
            transcendentals=heads * tokens * tokens // 2,
        ),
    )(group, doc_lengths, qkv)


def attend_back(group, doc_lengths, qkv, output, marks, cotangent, heads):
    tokens = qkv.shape[0]
    blocks = tokens // BLOCK
    columns = heads * BLOCK
    return pl.pallas_call(
        functools.partial(backward_kernel, heads),
        out_shape=jax.ShapeDtypeStruct(qkv.shape, jnp.bfloat16),
        in_specs=[SMEM, SMEM, ANY, ANY, ANY, ANY],
        out_specs=ANY,
        scratch_shapes=[
            pltpu.VMEM(qkv.shape, jnp.bfloat16),
            pltpu.VMEM(output.shape, jnp.bfloat16),
            pltpu.VMEM(marks.shape, jnp.bfloat16),
            pltpu.VMEM(cotangent.shape, jnp.bfloat16),
            pltpu.VMEM(qkv.shape, jnp.bfloat16),
            pltpu.VMEM((tokens, FEAT), jnp.bfloat16),
            pltpu.VMEM((blocks, FEAT, BLOCK), jnp.bfloat16),
            pltpu.VMEM((columns, 2 * FEAT), jnp.bfloat16),
            pltpu.VMEM((columns, 2 * FEAT), jnp.bfloat16),
            pltpu.VMEM((2 * FEAT, columns), jnp.bfloat16),
            pltpu.VMEM((2 * FEAT, columns), jnp.bfloat16),
            pltpu.VMEM((FEAT, columns), jnp.float32),
            pltpu.VMEM((tokens, FEAT), jnp.float32),
            pltpu.VMEM((tokens, FEAT), jnp.float32),
            pltpu.SemaphoreType.DMA((4, blocks)),
            pltpu.SemaphoreType.DMA((2, blocks)),
        ],
        compiler_params=LARGE,
        cost_estimate=pl.CostEstimate(
            flops=5 * 2 * heads * tokens * tokens * FEAT,
            bytes_accessed=7 * 2**20,
            transcendentals=heads * tokens * tokens // 2,
        ),
    )(group, doc_lengths, qkv, output, marks, cotangent)


def prologue_kernel(
    repeats,
    q_hbm,
    k_hbm,
    v_hbm,
    cot_hbm,
    qkv_hbm,
    by_device_hbm,
    q_ref,
    k_ref,
    v_ref,
    cot_ref,
    qkv_ref,
    by_device_ref,
    in_sems,
    out_sems,
):
    devices, tokens, width = by_device_hbm.shape
    parts = in_sems.shape[1]
    span = tokens // parts
    arrivals = [
        [
            pltpu.make_async_copy(
                source.at[part * span : (part + 1) * span, :],
                target.at[part * span : (part + 1) * span, :],
                in_sems.at[n, part],
            )
            for part in range(parts)
        ]
        for n, (source, target) in enumerate(
            ((q_hbm, q_ref), (k_hbm, k_ref), (v_hbm, v_ref), (cot_hbm, cot_ref))
        )
    ]
    for group in arrivals:
        for arrival in group:
            arrival.start()
    for group in arrivals[:3]:
        for arrival in group:
            arrival.wait()
    departures = []
    for device in range(devices):
        shared = slice(device // repeats * FEAT, (device // repeats + 1) * FEAT)
        qkv_ref[device, :, :width] = q_ref[:, device * width : (device + 1) * width]
        qkv_ref[device, :, width : width + FEAT] = k_ref[:, shared]
        qkv_ref[device, :, width + FEAT :] = v_ref[:, shared]
        departures.append(
            pltpu.make_async_copy(qkv_ref.at[device], qkv_hbm.at[device], out_sems.at[0, device])
        )
        departures[-1].start()
    for arrival in arrivals[3]:
        arrival.wait()
    for device in range(devices):
        by_device_ref[device] = cot_ref[:, device * width : (device + 1) * width]
        departures.append(
            pltpu.make_async_copy(
                by_device_ref.at[device], by_device_hbm.at[device], out_sems.at[1, device]
            )
        )
        departures[-1].start()
    for departure in departures:
        departure.wait()


def by_device(queries, key_vectors, value_vectors, grad_out, devices):
    tokens = queries.shape[0]
    width = queries.shape[1] // devices
    outs = (
        jax.ShapeDtypeStruct((devices, tokens, width + 2 * FEAT), jnp.bfloat16),
        jax.ShapeDtypeStruct((devices, tokens, width), jnp.bfloat16),
    )
    arrays = (queries, key_vectors, value_vectors, grad_out, *outs)
    return pl.pallas_call(
        functools.partial(prologue_kernel, devices // KV_HEADS),
        out_shape=outs,
        in_specs=[ANY] * 4,
        out_specs=(ANY, ANY),
        scratch_shapes=[pltpu.VMEM(array.shape, array.dtype) for array in arrays]
        + [pltpu.SemaphoreType.DMA((4, 4)), pltpu.SemaphoreType.DMA((2, devices))],
        compiler_params=LARGE,
    )(queries, key_vectors, value_vectors, grad_out)


def epilogue_kernel(repeats, grads_ref, attn_ref, out_ref, dq_ref, dk_ref, dv_ref):
    devices, _, width = attn_ref.shape
    for device in range(devices):
        cols = slice(device * width, (device + 1) * width)
        out_ref[:, cols] = attn_ref[device]
        dq_ref[:, cols] = grads_ref[device, :, :width]
    for head in range(devices // repeats):
        cols = slice(head * FEAT, (head + 1) * FEAT)
        for ref, at in ((dk_ref, width), (dv_ref, width + FEAT)):
            parts = [
                grads_ref[head * repeats + part, :, at : at + FEAT].astype(jnp.float32)
                for part in range(repeats)
            ]
            ref[:, cols] = functools.reduce(jnp.add, parts).astype(jnp.bfloat16)


def by_token(grads, attn):
    devices, tokens, width = attn.shape
    wide = jax.ShapeDtypeStruct((tokens, devices * width), jnp.bfloat16)
    narrow = jax.ShapeDtypeStruct((tokens, KV_HEADS * FEAT), jnp.bfloat16)
    return pl.pallas_call(
        functools.partial(epilogue_kernel, devices // KV_HEADS),
        out_shape=(wide, wide, narrow, narrow),
        in_specs=[VMEM] * 2,
        out_specs=(VMEM,) * 4,
        compiler_params=SMALL,
    )(grads, attn)


def over_heads(block):
    return lax.all_to_all(block, "head", split_axis=0, concat_axis=0, tiled=True)


def along_rows(block, distance):
    count = lax.axis_size("grp")
    return lax.ppermute(block, "grp", [(i, (i + distance) % count) for i in range(count)])


def first_part(shift, cotangent):
    return along_rows(cotangent, -shift)


def last_part(shift, attn):
    return along_rows(attn, shift)


def shards(queries, key_vectors, value_vectors, grad_out, doc_lengths, parcel_shift):
    group = lax.axis_index("grp").astype(jnp.int32).reshape(1)
    devices = lax.axis_size("head")
    heads = HEADS // devices
    shifts = range(1, lax.axis_size("grp"))
    choice = parcel_shift[0] - 1

    qkv, cotangent = by_device(queries, key_vectors, value_vectors, grad_out, devices)
    shape = cotangent.shape
    qkv = over_heads(qkv)
    cotangent = lax.switch(choice, [functools.partial(first_part, s) for s in shifts], cotangent)
    qkv, cotangent = lax.optimization_barrier((qkv, cotangent))
    qkv = qkv.reshape(shape[0] * shape[1], -1)
    cotangent = over_heads(cotangent)
    output, marks = attend(group, doc_lengths, qkv, heads)
    attn, cotangent = lax.optimization_barrier((output.reshape(shape), cotangent))
    attn = over_heads(attn)
    cotangent = cotangent.reshape(output.shape)
    grads = attend_back(group, doc_lengths, qkv, output, marks, cotangent, heads)
    grads = grads.reshape(shape[0], shape[1], -1)
    grads, attn = lax.optimization_barrier((grads, attn))
    grads = over_heads(grads)
    attn = lax.switch(choice, [functools.partial(last_part, s) for s in shifts], attn)
    return by_token(grads, attn)


def solution(mesh):
    split = P(("grp", "head"), None)
    return jax.shard_map(
        shards,
        mesh=mesh,
        in_specs=(split, split, split, split, P(), P()),
        out_specs=(split, split, split, split),
        check_vma=False,
    )
```

```python
import functools
import math

import jax
import jax.numpy as jnp
from jax import lax
from jax.experimental import pallas as pl
from jax.experimental.pallas import tpu as pltpu
from jax.sharding import PartitionSpec as P

HEADS = 32
KV_HEADS = 8
FEAT = 128
DOCS = 3
BLOCK = 512
SCALING = FEAT**-0.5
LOG2_SCALING = SCALING * math.log2(math.e)
EXCLUDED = -1e30


def dot(a, b):
    return jnp.dot(a, b, preferred_element_type=jnp.float32)


def rows(block):
    return pl.ds(pl.multiple_of(block * BLOCK, BLOCK), BLOCK)


def start_of(position, first, second):
    return jnp.where(position < first, 0, jnp.where(position < second, first, second))


def lanes_and_documents(block, first, second):
    lane = lax.broadcasted_iota(jnp.int32, (BLOCK, FEAT), 1)
    position = block * BLOCK + lax.broadcasted_iota(jnp.int32, (BLOCK, FEAT), 0)
    return lane, (position >= first).astype(jnp.int32) + (position >= second).astype(jnp.int32)


def in_lanes(lane, column):
    high = column.astype(jnp.bfloat16).astype(jnp.float32)
    middle = (column - high).astype(jnp.bfloat16).astype(jnp.float32)
    low = column - high - middle
    picked = jnp.where(lane == DOCS, high, jnp.where(lane == DOCS + 1, middle, low))
    return jnp.where((lane >= DOCS) & (lane < DOCS + 3), picked, 0.0)


def fill_key_marks(marks_ref, block, first, second):
    lane, document = lanes_and_documents(block, first, second)
    marked = (lane == document) | ((lane >= DOCS) & (lane < DOCS + 3))
    marks_ref[rows(block), :] = marked.astype(jnp.float32).astype(jnp.bfloat16)


def causal(values, other):
    key = lax.broadcasted_iota(jnp.int32, values.shape, 0)
    query = lax.rem(lax.broadcasted_iota(jnp.int32, values.shape, 1), BLOCK)
    return jnp.where(key <= query, values, other)


def causal_rows(values):
    query = lax.rem(lax.broadcasted_iota(jnp.int32, values.shape, 0), BLOCK)
    key = lax.broadcasted_iota(jnp.int32, values.shape, 1)
    return jnp.where(key <= query, values, EXCLUDED)


def folded(combine, values):
    parts = [values[:, at : at + FEAT] for at in range(0, values.shape[1], FEAT)]
    return functools.reduce(combine, parts)


def forward_kernel(
    heads,
    group_ref,
    lengths_ref,
    qkv_hbm,
    out_hbm,
    marks_hbm,
    qkv_ref,
    out_ref,
    marks_ref,
    kt_ref,
    query_ref,
    scores_ref,
    top_ref,
    total_ref,
    acc_ref,
    in_sems,
    out_sems,
):
    blocks = qkv_ref.shape[0] // BLOCK
    group = group_ref[0]
    first = lengths_ref[group, 0]
    second = first + lengths_ref[group, 1]
    key_cols = slice(heads * FEAT, (heads + 1) * FEAT)
    value_cols = slice((heads + 1) * FEAT, (heads + 2) * FEAT)

    def arrival(block):
        here = rows(block)
        return pltpu.make_async_copy(qkv_hbm.at[here, :], qkv_ref.at[here, :], in_sems.at[block])

    def departures(block):
        here = rows(block)
        return (
            pltpu.make_async_copy(out_ref.at[here, :], out_hbm.at[here, :], out_sems.at[0, block]),
            pltpu.make_async_copy(
                marks_ref.at[here, :], marks_hbm.at[here, :], out_sems.at[1, block]
            ),
        )

    for block in range(blocks):
        arrival(block).start()

    def one_query_block(block, _):
        arrival(block).wait()
        kt_ref[block, :FEAT, :] = qkv_ref[rows(block), key_cols].T
        kind = lax.broadcasted_iota(jnp.int32, (FEAT, BLOCK), 0)
        position = block * BLOCK + lax.broadcasted_iota(jnp.int32, (FEAT, BLOCK), 1)
        document = (position >= first).astype(jnp.int32) + (position >= second).astype(jnp.int32)
        kt_ref[block, FEAT:, :] = (kind == document).astype(jnp.float32).astype(jnp.bfloat16)
        lane, document = lanes_and_documents(block, first, second)
        marks = jnp.where((lane != document) & (lane < DOCS), EXCLUDED, 0.0)
        for h in range(heads):
            query_ref[h * BLOCK : (h + 1) * BLOCK, :FEAT] = qkv_ref[
                rows(block), h * FEAT : (h + 1) * FEAT
            ]
            query_ref[h * BLOCK : (h + 1) * BLOCK, FEAT:] = marks.astype(jnp.bfloat16)
        lowest = start_of(block * BLOCK, first, second) // BLOCK
        scores = causal_rows(dot(query_ref[...], kt_ref[block]))
        scores_ref[block] = scores
        top_ref[...] = folded(jnp.maximum, scores)

        def earlier(key_block, _):
            scores = dot(query_ref[...], kt_ref[key_block])
            scores_ref[key_block] = scores
            top_ref[...] = jnp.maximum(top_ref[...], folded(jnp.maximum, scores))
            return 0

        lax.fori_loop(lowest, block, earlier, 0)
        top = jnp.max(top_ref[...], axis=1, keepdims=True) * LOG2_SCALING
        top_ref[...] = jnp.broadcast_to(top, top_ref.shape)
        total_ref[...] = jnp.zeros_like(total_ref)
        acc_ref[...] = jnp.zeros_like(acc_ref)

        def weigh(key_block, _):
            top = top_ref[...]
            exponent = jnp.exp2(
                scores_ref[key_block] * LOG2_SCALING - jnp.concatenate([top] * (BLOCK // FEAT), axis=1)
            )
            total_ref[...] += folded(jnp.add, exponent)
            acc_ref[...] += dot(exponent.astype(jnp.bfloat16), qkv_ref[rows(key_block), value_cols])
            return 0

        lax.fori_loop(lowest, block + 1, weigh, 0)
        total = jnp.sum(total_ref[...], axis=1, keepdims=True)
        output = (acc_ref[...] * (1.0 / total)).astype(jnp.bfloat16)
        lse = (top + jnp.log2(total)) * (-1.0 / LOG2_SCALING)
        for h in range(heads):
            here = slice(h * BLOCK, (h + 1) * BLOCK)
            out_ref[rows(block), h * FEAT : (h + 1) * FEAT] = output[here]
            marks_ref[rows(block), h * FEAT : (h + 1) * FEAT] = (
                marks + in_lanes(lane, lse[here])
            ).astype(jnp.bfloat16)
        for departure in departures(block):
            departure.start()
        return 0

    lax.fori_loop(0, blocks, one_query_block, 0)
    for block in range(blocks):
        for departure in departures(block):
            departure.wait()


def backward_kernel(
    heads,
    group_ref,
    lengths_ref,
    qkv_hbm,
    out_hbm,
    marks_hbm,
    cot_hbm,
    grad_hbm,
    qkv_ref,
    out_ref,
    marks_ref,
    cot_ref,
    grad_ref,
    key_marks_ref,
    kt_ref,
    query_ref,
    cotangent_ref,
    query_t_ref,
    cotangent_t_ref,
    dq_ref,
    dk_ref,
    dv_ref,
    in_sems,
    out_sems,
):
    blocks = qkv_ref.shape[0] // BLOCK
    group = group_ref[0]
    first = lengths_ref[group, 0]
    second = first + lengths_ref[group, 1]
    query_cols = slice(0, heads * FEAT)
    key_cols = slice(heads * FEAT, (heads + 1) * FEAT)
    value_cols = slice((heads + 1) * FEAT, (heads + 2) * FEAT)
    shared_cols = slice(heads * FEAT, (heads + 2) * FEAT)

    def arrivals(block):
        here = rows(block)
        pairs = ((qkv_hbm, qkv_ref), (out_hbm, out_ref), (marks_hbm, marks_ref), (cot_hbm, cot_ref))
        return [
            pltpu.make_async_copy(source.at[here, :], target.at[here, :], in_sems.at[n, block])
            for n, (source, target) in enumerate(pairs)
        ]

    def departure(block, cols, which):
        here = rows(block)
        return pltpu.make_async_copy(
            grad_ref.at[here, cols], grad_hbm.at[here, cols], out_sems.at[which, block]
        )

    for block in range(blocks):
        for arrival in arrivals(block):
            arrival.start()

    def one_query_block(block, _):
        for arrival in arrivals(block):
            arrival.wait()
        fill_key_marks(key_marks_ref, block, first, second)
        kt_ref[block] = qkv_ref[rows(block), key_cols].T
        dk_ref[rows(block), :] = jnp.zeros((BLOCK, FEAT), jnp.float32)
        dv_ref[rows(block), :] = jnp.zeros((BLOCK, FEAT), jnp.float32)
        lane = lax.broadcasted_iota(jnp.int32, (BLOCK, FEAT), 1)
        for h in range(heads):
            here = slice(h * BLOCK, (h + 1) * BLOCK)
            cols = slice(h * FEAT, (h + 1) * FEAT)
            query_ref[here, :FEAT] = qkv_ref[rows(block), cols]
            query_ref[here, FEAT:] = marks_ref[rows(block), cols]
            cotangent = cot_ref[rows(block), cols]
            product = cotangent.astype(jnp.float32) * out_ref[rows(block), cols].astype(jnp.float32)
            delta = jnp.sum(product, axis=1, keepdims=True)
            cotangent_ref[here, :FEAT] = cotangent
            cotangent_ref[here, FEAT:] = in_lanes(lane, -delta).astype(jnp.bfloat16)
        query_t_ref[...] = query_ref[...].T
        cotangent_t_ref[...] = cotangent_ref[...].T
        lowest = start_of(block * BLOCK, first, second) // BLOCK
        dq_ref[...] = jnp.zeros_like(dq_ref)

        def one_key_block(key_block, diagonal):
            here = rows(key_block)
            key_marks = key_marks_ref[here, :]
            keys = jnp.concatenate([qkv_ref[here, key_cols], key_marks], axis=1)
            values = jnp.concatenate([qkv_ref[here, value_cols], key_marks], axis=1)
            probs = jnp.exp2(dot(keys, query_t_ref[...]) * LOG2_SCALING)
            if diagonal:
                probs = causal(probs, 0.0)
            grad_score = probs * dot(values, cotangent_t_ref[...])
            grad_score = grad_score.astype(jnp.bfloat16)
            dv_ref[here, :] += dot(probs.astype(jnp.bfloat16), cotangent_ref[:, :FEAT])
            dk_ref[here, :] += dot(grad_score, query_ref[:, :FEAT])
            dq_ref[...] += dot(kt_ref[key_block], grad_score)

        def earlier(key_block, _):
            one_key_block(key_block, False)
            return 0

        lax.fori_loop(lowest, block, earlier, 0)
        one_key_block(block, True)
        dq = (dq_ref[...] * SCALING).T.astype(jnp.bfloat16)
        for h in range(heads):
            grad_ref[rows(block), h * FEAT : (h + 1) * FEAT] = dq[h * BLOCK : (h + 1) * BLOCK]
        departure(block, query_cols, 0).start()
        return 0

    lax.fori_loop(0, blocks, one_query_block, 0)

    def finish(block, _):
        grad_ref[rows(block), key_cols] = (dk_ref[rows(block), :] * SCALING).astype(jnp.bfloat16)
        grad_ref[rows(block), value_cols] = dv_ref[rows(block), :].astype(jnp.bfloat16)
        departure(block, shared_cols, 1).start()
        return 0

    lax.fori_loop(0, blocks, finish, 0)
    for block in range(blocks):
        departure(block, query_cols, 0).wait()
        departure(block, shared_cols, 1).wait()


SMEM = pl.BlockSpec(memory_space=pltpu.SMEM)
VMEM = pl.BlockSpec(memory_space=pltpu.VMEM)
ANY = pl.BlockSpec(memory_space=pl.ANY)
SMALL = pltpu.CompilerParams(vmem_limit_bytes=32 * 2**20)
LARGE = pltpu.CompilerParams(vmem_limit_bytes=56 * 2**20)


def attend(group, doc_lengths, qkv, heads):
    tokens = qkv.shape[0]
    blocks = tokens // BLOCK
    columns = heads * BLOCK
    wide = jax.ShapeDtypeStruct((tokens, heads * FEAT), jnp.bfloat16)
    return pl.pallas_call(
        functools.partial(forward_kernel, heads),
        out_shape=(wide, wide),
        in_specs=[SMEM, SMEM, ANY],
        out_specs=(ANY, ANY),
        scratch_shapes=[
            pltpu.VMEM(qkv.shape, jnp.bfloat16),
            pltpu.VMEM(wide.shape, jnp.bfloat16),
            pltpu.VMEM(wide.shape, jnp.bfloat16),
            pltpu.VMEM((blocks, 2 * FEAT, BLOCK), jnp.bfloat16),
            pltpu.VMEM((columns, 2 * FEAT), jnp.bfloat16),
            pltpu.VMEM((blocks, columns, BLOCK), jnp.float32),
            pltpu.VMEM((columns, FEAT), jnp.float32),
            pltpu.VMEM((columns, FEAT), jnp.float32),
            pltpu.VMEM((columns, FEAT), jnp.float32),
            pltpu.SemaphoreType.DMA((blocks,)),
            pltpu.SemaphoreType.DMA((2, blocks)),
        ],
        compiler_params=LARGE,
        cost_estimate=pl.CostEstimate(
            flops=2 * 2 * heads * tokens * tokens * FEAT,
            bytes_accessed=4 * 2**20,
            transcendentals=heads * tokens * tokens // 2,
        ),
    )(group, doc_lengths, qkv)


def attend_back(group, doc_lengths, qkv, output, marks, cotangent, heads):
    tokens = qkv.shape[0]
    blocks = tokens // BLOCK
    columns = heads * BLOCK
    return pl.pallas_call(
        functools.partial(backward_kernel, heads),
        out_shape=jax.ShapeDtypeStruct(qkv.shape, jnp.bfloat16),
        in_specs=[SMEM, SMEM, ANY, ANY, ANY, ANY],
        out_specs=ANY,
        scratch_shapes=[
            pltpu.VMEM(qkv.shape, jnp.bfloat16),
            pltpu.VMEM(output.shape, jnp.bfloat16),
            pltpu.VMEM(marks.shape, jnp.bfloat16),
            pltpu.VMEM(cotangent.shape, jnp.bfloat16),
            pltpu.VMEM(qkv.shape, jnp.bfloat16),
            pltpu.VMEM((tokens, FEAT), jnp.bfloat16),
            pltpu.VMEM((blocks, FEAT, BLOCK), jnp.bfloat16),
            pltpu.VMEM((columns, 2 * FEAT), jnp.bfloat16),
            pltpu.VMEM((columns, 2 * FEAT), jnp.bfloat16),
            pltpu.VMEM((2 * FEAT, columns), jnp.bfloat16),
            pltpu.VMEM((2 * FEAT, columns), jnp.bfloat16),
            pltpu.VMEM((FEAT, columns), jnp.float32),
            pltpu.VMEM((tokens, FEAT), jnp.float32),
            pltpu.VMEM((tokens, FEAT), jnp.float32),
            pltpu.SemaphoreType.DMA((4, blocks)),
            pltpu.SemaphoreType.DMA((2, blocks)),
        ],
        compiler_params=LARGE,
        cost_estimate=pl.CostEstimate(
            flops=5 * 2 * heads * tokens * tokens * FEAT,
            bytes_accessed=7 * 2**20,
            transcendentals=heads * tokens * tokens // 2,
        ),
    )(group, doc_lengths, qkv, output, marks, cotangent)


def prologue_kernel(
    repeats,
    q_hbm,
    k_hbm,
    v_hbm,
    cot_hbm,
    qkv_hbm,
    by_device_hbm,
    q_ref,
    k_ref,
    v_ref,
    cot_ref,
    qkv_ref,
    by_device_ref,
    in_sems,
    out_sems,
):
    devices, tokens, width = by_device_hbm.shape
    parts = in_sems.shape[1]
    span = tokens // parts
    arrivals = [
        [
            pltpu.make_async_copy(
                source.at[part * span : (part + 1) * span, :],
                target.at[part * span : (part + 1) * span, :],
                in_sems.at[n, part],
            )
            for part in range(parts)
        ]
        for n, (source, target) in enumerate(
            ((q_hbm, q_ref), (k_hbm, k_ref), (v_hbm, v_ref), (cot_hbm, cot_ref))
        )
    ]
    for group in arrivals:
        for arrival in group:
            arrival.start()
    for group in arrivals[:3]:
        for arrival in group:
            arrival.wait()
    departures = []
    for device in range(devices):
        shared = slice(device // repeats * FEAT, (device // repeats + 1) * FEAT)
        qkv_ref[device, :, :width] = q_ref[:, device * width : (device + 1) * width]
        qkv_ref[device, :, width : width + FEAT] = k_ref[:, shared]
        qkv_ref[device, :, width + FEAT :] = v_ref[:, shared]
        departures.append(
            pltpu.make_async_copy(qkv_ref.at[device], qkv_hbm.at[device], out_sems.at[0, device])
        )
        departures[-1].start()
    for arrival in arrivals[3]:
        arrival.wait()
    for device in range(devices):
        by_device_ref[device] = cot_ref[:, device * width : (device + 1) * width]
        departures.append(
            pltpu.make_async_copy(
                by_device_ref.at[device], by_device_hbm.at[device], out_sems.at[1, device]
            )
        )
        departures[-1].start()
    for departure in departures:
        departure.wait()


def by_device(queries, key_vectors, value_vectors, grad_out, devices):
    tokens = queries.shape[0]
    width = queries.shape[1] // devices
    outs = (
        jax.ShapeDtypeStruct((devices, tokens, width + 2 * FEAT), jnp.bfloat16),
        jax.ShapeDtypeStruct((devices, tokens, width), jnp.bfloat16),
    )
    arrays = (queries, key_vectors, value_vectors, grad_out, *outs)
    return pl.pallas_call(
        functools.partial(prologue_kernel, devices // KV_HEADS),
        out_shape=outs,
        in_specs=[ANY] * 4,
        out_specs=(ANY, ANY),
        scratch_shapes=[pltpu.VMEM(array.shape, array.dtype) for array in arrays]
        + [pltpu.SemaphoreType.DMA((4, 4)), pltpu.SemaphoreType.DMA((2, devices))],
        compiler_params=LARGE,
    )(queries, key_vectors, value_vectors, grad_out)


def epilogue_kernel(repeats, grads_ref, attn_ref, out_ref, dq_ref, dk_ref, dv_ref):
    devices, _, width = attn_ref.shape
    for device in range(devices):
        cols = slice(device * width, (device + 1) * width)
        out_ref[:, cols] = attn_ref[device]
        dq_ref[:, cols] = grads_ref[device, :, :width]
    for head in range(devices // repeats):
        cols = slice(head * FEAT, (head + 1) * FEAT)
        for ref, at in ((dk_ref, width), (dv_ref, width + FEAT)):
            parts = [
                grads_ref[head * repeats + part, :, at : at + FEAT].astype(jnp.float32)
                for part in range(repeats)
            ]
            ref[:, cols] = functools.reduce(jnp.add, parts).astype(jnp.bfloat16)


def by_token(grads, attn):
    devices, tokens, width = attn.shape
    wide = jax.ShapeDtypeStruct((tokens, devices * width), jnp.bfloat16)
    narrow = jax.ShapeDtypeStruct((tokens, KV_HEADS * FEAT), jnp.bfloat16)
    return pl.pallas_call(
        functools.partial(epilogue_kernel, devices // KV_HEADS),
        out_shape=(wide, wide, narrow, narrow),
        in_specs=[VMEM] * 2,
        out_specs=(VMEM,) * 4,
        compiler_params=SMALL,
    )(grads, attn)


def over_heads(block):
    return lax.all_to_all(block, "head", split_axis=0, concat_axis=0, tiled=True)


def hop(block, distance):
    count = lax.axis_size("grp")
    return lax.ppermute(block, "grp", [(i, (i + distance) % count) for i in range(count)])


LONG_WAY = {5: 4, 6: 5}


def along_rows(block, distance, split=False):
    count = lax.axis_size("grp")
    distance %= count
    short = distance if 2 * distance <= count else distance - count
    parts = LONG_WAY.get(abs(short), 0) * block.shape[0] // 16
    if not parts or not split:
        return hop(block, short)
    long = short - count if short > 0 else short + count
    far = hop(block[:parts], long // 2)
    near = hop(block[parts:], short)
    far = hop(far, long - long // 2)
    return jnp.concatenate([far, near], axis=0)


def first_part(shift, cotangent):
    return along_rows(cotangent, -shift)


def last_part(shift, attn):
    return along_rows(attn, shift, split=True)


def shards(queries, key_vectors, value_vectors, grad_out, doc_lengths, parcel_shift):
    group = lax.axis_index("grp").astype(jnp.int32).reshape(1)
    devices = lax.axis_size("head")
    heads = HEADS // devices
    shifts = range(1, lax.axis_size("grp"))
    choice = parcel_shift[0] - 1

    qkv, cotangent = by_device(queries, key_vectors, value_vectors, grad_out, devices)
    shape = cotangent.shape
    qkv = over_heads(qkv)
    cotangent = lax.switch(choice, [functools.partial(first_part, s) for s in shifts], cotangent)
    qkv, cotangent = lax.optimization_barrier((qkv, cotangent))
    qkv = qkv.reshape(shape[0] * shape[1], -1)
    cotangent = over_heads(cotangent)
    output, marks = attend(group, doc_lengths, qkv, heads)
    attn, cotangent = lax.optimization_barrier((output.reshape(shape), cotangent))
    attn = over_heads(attn)
    cotangent = cotangent.reshape(output.shape)
    grads = attend_back(group, doc_lengths, qkv, output, marks, cotangent, heads)
    grads = grads.reshape(shape[0], shape[1], -1)
    grads, attn = lax.optimization_barrier((grads, attn))
    grads = over_heads(grads)
    attn = lax.switch(choice, [functools.partial(last_part, s) for s in shifts], attn)
    return by_token(grads, attn)


def solution(mesh):
    split = P(("grp", "head"), None)
    return jax.shard_map(
        shards,
        mesh=mesh,
        in_specs=(split, split, split, split, P(), P()),
        out_specs=(split, split, split, split),
        check_vma=False,
    )
```

```python
import functools
import math

import jax
import jax.numpy as jnp
from jax import lax
from jax.experimental import pallas as pl
from jax.experimental.pallas import tpu as pltpu
from jax.sharding import PartitionSpec as P

HEADS = 32
KV_HEADS = 8
FEAT = 128
DOCS = 3
BLOCK = 512
SCALING = FEAT**-0.5
LOG2_SCALING = SCALING * math.log2(math.e)
EXCLUDED = -1e30


def dot(a, b):
    return jnp.dot(a, b, preferred_element_type=jnp.float32)


def rows(block):
    return pl.ds(pl.multiple_of(block * BLOCK, BLOCK), BLOCK)


def start_of(position, first, second):
    return jnp.where(position < first, 0, jnp.where(position < second, first, second))


def lanes_and_documents(block, first, second):
    lane = lax.broadcasted_iota(jnp.int32, (BLOCK, FEAT), 1)
    position = block * BLOCK + lax.broadcasted_iota(jnp.int32, (BLOCK, FEAT), 0)
    return lane, (position >= first).astype(jnp.int32) + (position >= second).astype(jnp.int32)


def in_lanes(lane, column):
    high = column.astype(jnp.bfloat16).astype(jnp.float32)
    middle = (column - high).astype(jnp.bfloat16).astype(jnp.float32)
    low = column - high - middle
    picked = jnp.where(lane == DOCS, high, jnp.where(lane == DOCS + 1, middle, low))
    return jnp.where((lane >= DOCS) & (lane < DOCS + 3), picked, 0.0)


def fill_key_marks(marks_ref, block, first, second):
    lane, document = lanes_and_documents(block, first, second)
    marked = (lane == document) | ((lane >= DOCS) & (lane < DOCS + 3))
    marks_ref[rows(block), :] = marked.astype(jnp.float32).astype(jnp.bfloat16)


def causal_rows(values):
    query = lax.rem(lax.broadcasted_iota(jnp.int32, values.shape, 0), BLOCK)
    key = lax.broadcasted_iota(jnp.int32, values.shape, 1)
    return jnp.where(key <= query, values, EXCLUDED)


def folded(combine, values):
    parts = [values[:, at : at + FEAT] for at in range(0, values.shape[1], FEAT)]
    return functools.reduce(combine, parts)


def forward_kernel(
    heads,
    group_ref,
    lengths_ref,
    qkv_hbm,
    out_hbm,
    marks_hbm,
    qkv_ref,
    out_ref,
    marks_ref,
    kt_ref,
    query_ref,
    scores_ref,
    top_ref,
    total_ref,
    acc_ref,
    in_sems,
    out_sems,
):
    blocks = qkv_ref.shape[0] // BLOCK
    group = group_ref[0]
    first = lengths_ref[group, 0]
    second = first + lengths_ref[group, 1]
    key_cols = slice(heads * FEAT, (heads + 1) * FEAT)
    value_cols = slice((heads + 1) * FEAT, (heads + 2) * FEAT)

    def arrival(block):
        here = rows(block)
        return pltpu.make_async_copy(qkv_hbm.at[here, :], qkv_ref.at[here, :], in_sems.at[block])

    def departures(block):
        here = rows(block)
        return (
            pltpu.make_async_copy(out_ref.at[here, :], out_hbm.at[here, :], out_sems.at[0, block]),
            pltpu.make_async_copy(
                marks_ref.at[here, :], marks_hbm.at[here, :], out_sems.at[1, block]
            ),
        )

    for block in range(blocks):
        arrival(block).start()

    def one_query_block(block, _):
        arrival(block).wait()
        kt_ref[block, :FEAT, :] = qkv_ref[rows(block), key_cols].T
        kind = lax.broadcasted_iota(jnp.int32, (FEAT, BLOCK), 0)
        position = block * BLOCK + lax.broadcasted_iota(jnp.int32, (FEAT, BLOCK), 1)
        document = (position >= first).astype(jnp.int32) + (position >= second).astype(jnp.int32)
        kt_ref[block, FEAT:, :] = (kind == document).astype(jnp.float32).astype(jnp.bfloat16)
        lane, document = lanes_and_documents(block, first, second)
        marks = jnp.where((lane != document) & (lane < DOCS), EXCLUDED, 0.0)
        for h in range(heads):
            query_ref[h * BLOCK : (h + 1) * BLOCK, :FEAT] = qkv_ref[
                rows(block), h * FEAT : (h + 1) * FEAT
            ]
            query_ref[h * BLOCK : (h + 1) * BLOCK, FEAT:] = marks.astype(jnp.bfloat16)
        lowest = start_of(block * BLOCK, first, second) // BLOCK
        scores = causal_rows(dot(query_ref[...], kt_ref[block]))
        scores_ref[block] = scores
        top_ref[...] = folded(jnp.maximum, scores)

        def earlier(key_block, _):
            scores = dot(query_ref[...], kt_ref[key_block])
            scores_ref[key_block] = scores
            top_ref[...] = jnp.maximum(top_ref[...], folded(jnp.maximum, scores))
            return 0

        lax.fori_loop(lowest, block, earlier, 0)
        top = jnp.max(top_ref[...], axis=1, keepdims=True) * LOG2_SCALING
        top_ref[...] = jnp.broadcast_to(top, top_ref.shape)
        total_ref[...] = jnp.zeros_like(total_ref)
        acc_ref[...] = jnp.zeros_like(acc_ref)

        def weigh(key_block, _):
            top = top_ref[...]
            exponent = jnp.exp2(
                scores_ref[key_block] * LOG2_SCALING - jnp.concatenate([top] * (BLOCK // FEAT), axis=1)
            )
            total_ref[...] += folded(jnp.add, exponent)
            acc_ref[...] += dot(exponent.astype(jnp.bfloat16), qkv_ref[rows(key_block), value_cols])
            return 0

        lax.fori_loop(lowest, block + 1, weigh, 0)
        total = jnp.sum(total_ref[...], axis=1, keepdims=True)
        output = (acc_ref[...] * (1.0 / total)).astype(jnp.bfloat16)
        lse = (top + jnp.log2(total)) * (-1.0 / LOG2_SCALING)
        for h in range(heads):
            here = slice(h * BLOCK, (h + 1) * BLOCK)
            out_ref[rows(block), h * FEAT : (h + 1) * FEAT] = output[here]
            marks_ref[rows(block), h * FEAT : (h + 1) * FEAT] = (
                marks + in_lanes(lane, lse[here])
            ).astype(jnp.bfloat16)
        for departure in departures(block):
            departure.start()
        return 0

    lax.fori_loop(0, blocks, one_query_block, 0)
    for block in range(blocks):
        for departure in departures(block):
            departure.wait()


def backward_kernel(
    heads,
    group_ref,
    lengths_ref,
    qkv_hbm,
    out_hbm,
    marks_hbm,
    cot_hbm,
    grad_hbm,
    qkv_ref,
    out_ref,
    marks_ref,
    cot_ref,
    grad_ref,
    key_marks_ref,
    kt_ref,
    query_ref,
    cotangent_ref,
    query_t_ref,
    cotangent_t_ref,
    dq_ref,
    dk_ref,
    dv_ref,
    in_sems,
    out_sems,
):
    blocks = qkv_ref.shape[0] // BLOCK
    group = group_ref[0]
    first = lengths_ref[group, 0]
    second = first + lengths_ref[group, 1]
    query_cols = slice(0, heads * FEAT)
    key_cols = slice(heads * FEAT, (heads + 1) * FEAT)
    value_cols = slice((heads + 1) * FEAT, (heads + 2) * FEAT)
    shared_cols = slice(heads * FEAT, (heads + 2) * FEAT)

    def arrivals(block):
        here = rows(block)
        pairs = ((qkv_hbm, qkv_ref), (out_hbm, out_ref), (marks_hbm, marks_ref), (cot_hbm, cot_ref))
        return [
            pltpu.make_async_copy(source.at[here, :], target.at[here, :], in_sems.at[n, block])
            for n, (source, target) in enumerate(pairs)
        ]

    def departure(block, cols, which):
        here = rows(block)
        return pltpu.make_async_copy(
            grad_ref.at[here, cols], grad_hbm.at[here, cols], out_sems.at[which, block]
        )

    for block in range(blocks):
        for arrival in arrivals(block):
            arrival.start()

    half = BLOCK // 2
    columns = heads * half

    def one_query_block(block, _):
        for arrival in arrivals(block):
            arrival.wait()
        fill_key_marks(key_marks_ref, block, first, second)
        kt_ref[block] = qkv_ref[rows(block), key_cols].T
        dk_ref[rows(block), :] = jnp.zeros((BLOCK, FEAT), jnp.float32)
        dv_ref[rows(block), :] = jnp.zeros((BLOCK, FEAT), jnp.float32)
        lane = lax.broadcasted_iota(jnp.int32, (half, FEAT), 1)
        places = []
        for part in range(2):
            for h in range(heads):
                at = (part * heads + h) * half
                here = pl.ds(pl.multiple_of(block * BLOCK + part * half, half), half)
                places.append((slice(at, at + half), here, slice(h * FEAT, (h + 1) * FEAT)))
        for at, here, cols in places:
            query_ref[at, :FEAT] = qkv_ref[here, cols]
            query_ref[at, FEAT:] = marks_ref[here, cols]
            cotangent = cot_ref[here, cols]
            product = cotangent.astype(jnp.float32) * out_ref[here, cols].astype(jnp.float32)
            delta = jnp.sum(product, axis=1, keepdims=True)
            cotangent_ref[at, :FEAT] = cotangent
            cotangent_ref[at, FEAT:] = in_lanes(lane, -delta).astype(jnp.bfloat16)
        query_t_ref[...] = query_ref[...].T
        cotangent_t_ref[...] = cotangent_ref[...].T
        dq_ref[...] = jnp.zeros_like(dq_ref)

        def add_part(key_block, keys_at, cols, diagonal):
            begin = pl.multiple_of(key_block * BLOCK + keys_at.start, half)
            here = pl.ds(begin, keys_at.stop - keys_at.start)
            key_marks = key_marks_ref[here, :]
            keys = jnp.concatenate([qkv_ref[here, key_cols], key_marks], axis=1)
            values = jnp.concatenate([qkv_ref[here, value_cols], key_marks], axis=1)
            probs = jnp.exp2(dot(keys, query_t_ref[:, cols]) * LOG2_SCALING)
            if diagonal:
                key = keys_at.start + lax.broadcasted_iota(jnp.int32, probs.shape, 0)
                column = cols.start + lax.broadcasted_iota(jnp.int32, probs.shape, 1)
                query = jnp.where(column < columns, 0, half) + lax.rem(column, half)
                probs = jnp.where(key <= query, probs, 0.0)
            grad_score = probs * dot(values, cotangent_t_ref[:, cols])
            grad_score = grad_score.astype(jnp.bfloat16)
            dv_ref[here, :] += dot(probs.astype(jnp.bfloat16), cotangent_ref[cols, :FEAT])
            dk_ref[here, :] += dot(grad_score, query_ref[cols, :FEAT])
            dq_ref[:, cols] += dot(kt_ref[key_block, :, keys_at], grad_score)

        def for_first_half(key_block, _):
            add_part(key_block, slice(0, BLOCK), slice(0, columns), False)
            return 0

        def for_both(key_block, _):
            add_part(key_block, slice(0, BLOCK), slice(0, 2 * columns), False)
            return 0

        lowest = start_of(block * BLOCK, first, second) // BLOCK
        lowest_of_both = start_of(block * BLOCK + half, first, second) // BLOCK
        lax.fori_loop(lowest, lowest_of_both, for_first_half, 0)
        lax.fori_loop(lowest_of_both, block, for_both, 0)
        add_part(block, slice(0, half), slice(0, 2 * columns), True)
        add_part(block, slice(half, BLOCK), slice(columns, 2 * columns), True)
        dq = (dq_ref[...] * SCALING).T.astype(jnp.bfloat16)
        for at, here, cols in places:
            grad_ref[here, cols] = dq[at]
        departure(block, query_cols, 0).start()
        return 0

    lax.fori_loop(0, blocks, one_query_block, 0)

    def finish(block, _):
        grad_ref[rows(block), key_cols] = (dk_ref[rows(block), :] * SCALING).astype(jnp.bfloat16)
        grad_ref[rows(block), value_cols] = dv_ref[rows(block), :].astype(jnp.bfloat16)
        departure(block, shared_cols, 1).start()
        return 0

    lax.fori_loop(0, blocks, finish, 0)
    for block in range(blocks):
        departure(block, query_cols, 0).wait()
        departure(block, shared_cols, 1).wait()


SMEM = pl.BlockSpec(memory_space=pltpu.SMEM)
VMEM = pl.BlockSpec(memory_space=pltpu.VMEM)
ANY = pl.BlockSpec(memory_space=pl.ANY)
SMALL = pltpu.CompilerParams(vmem_limit_bytes=32 * 2**20)
LARGE = pltpu.CompilerParams(vmem_limit_bytes=56 * 2**20)


def attend(group, doc_lengths, qkv, heads):
    tokens = qkv.shape[0]
    blocks = tokens // BLOCK
    columns = heads * BLOCK
    wide = jax.ShapeDtypeStruct((tokens, heads * FEAT), jnp.bfloat16)
    return pl.pallas_call(
        functools.partial(forward_kernel, heads),
        out_shape=(wide, wide),
        in_specs=[SMEM, SMEM, ANY],
        out_specs=(ANY, ANY),
        scratch_shapes=[
            pltpu.VMEM(qkv.shape, jnp.bfloat16),
            pltpu.VMEM(wide.shape, jnp.bfloat16),
            pltpu.VMEM(wide.shape, jnp.bfloat16),
            pltpu.VMEM((blocks, 2 * FEAT, BLOCK), jnp.bfloat16),
            pltpu.VMEM((columns, 2 * FEAT), jnp.bfloat16),
            pltpu.VMEM((blocks, columns, BLOCK), jnp.float32),
            pltpu.VMEM((columns, FEAT), jnp.float32),
            pltpu.VMEM((columns, FEAT), jnp.float32),
            pltpu.VMEM((columns, FEAT), jnp.float32),
            pltpu.SemaphoreType.DMA((blocks,)),
            pltpu.SemaphoreType.DMA((2, blocks)),
        ],
        compiler_params=LARGE,
        cost_estimate=pl.CostEstimate(
            flops=2 * 2 * heads * tokens * tokens * FEAT,
            bytes_accessed=4 * 2**20,
            transcendentals=heads * tokens * tokens // 2,
        ),
    )(group, doc_lengths, qkv)


def attend_back(group, doc_lengths, qkv, output, marks, cotangent, heads):
    tokens = qkv.shape[0]
    blocks = tokens // BLOCK
    columns = heads * BLOCK
    return pl.pallas_call(
        functools.partial(backward_kernel, heads),
        out_shape=jax.ShapeDtypeStruct(qkv.shape, jnp.bfloat16),
        in_specs=[SMEM, SMEM, ANY, ANY, ANY, ANY],
        out_specs=ANY,
        scratch_shapes=[
            pltpu.VMEM(qkv.shape, jnp.bfloat16),
            pltpu.VMEM(output.shape, jnp.bfloat16),
            pltpu.VMEM(marks.shape, jnp.bfloat16),
            pltpu.VMEM(cotangent.shape, jnp.bfloat16),
            pltpu.VMEM(qkv.shape, jnp.bfloat16),
            pltpu.VMEM((tokens, FEAT), jnp.bfloat16),
            pltpu.VMEM((blocks, FEAT, BLOCK), jnp.bfloat16),
            pltpu.VMEM((columns, 2 * FEAT), jnp.bfloat16),
            pltpu.VMEM((columns, 2 * FEAT), jnp.bfloat16),
            pltpu.VMEM((2 * FEAT, columns), jnp.bfloat16),
            pltpu.VMEM((2 * FEAT, columns), jnp.bfloat16),
            pltpu.VMEM((FEAT, columns), jnp.float32),
            pltpu.VMEM((tokens, FEAT), jnp.float32),
            pltpu.VMEM((tokens, FEAT), jnp.float32),
            pltpu.SemaphoreType.DMA((4, blocks)),
            pltpu.SemaphoreType.DMA((2, blocks)),
        ],
        compiler_params=LARGE,
        cost_estimate=pl.CostEstimate(
            flops=5 * 2 * heads * tokens * tokens * FEAT,
            bytes_accessed=7 * 2**20,
            transcendentals=heads * tokens * tokens // 2,
        ),
    )(group, doc_lengths, qkv, output, marks, cotangent)


def prologue_kernel(
    repeats,
    q_hbm,
    k_hbm,
    v_hbm,
    cot_hbm,
    qkv_hbm,
    by_device_hbm,
    q_ref,
    k_ref,
    v_ref,
    cot_ref,
    qkv_ref,
    by_device_ref,
    in_sems,
    out_sems,
):
    devices, tokens, width = by_device_hbm.shape
    parts = in_sems.shape[1]
    span = tokens // parts
    arrivals = [
        [
            pltpu.make_async_copy(
                source.at[part * span : (part + 1) * span, :],
                target.at[part * span : (part + 1) * span, :],
                in_sems.at[n, part],
            )
            for part in range(parts)
        ]
        for n, (source, target) in enumerate(
            ((q_hbm, q_ref), (k_hbm, k_ref), (v_hbm, v_ref), (cot_hbm, cot_ref))
        )
    ]
    for group in arrivals:
        for arrival in group:
            arrival.start()
    for group in arrivals[:3]:
        for arrival in group:
            arrival.wait()
    departures = []
    for device in range(devices):
        shared = slice(device // repeats * FEAT, (device // repeats + 1) * FEAT)
        qkv_ref[device, :, :width] = q_ref[:, device * width : (device + 1) * width]
        qkv_ref[device, :, width : width + FEAT] = k_ref[:, shared]
        qkv_ref[device, :, width + FEAT :] = v_ref[:, shared]
        departures.append(
            pltpu.make_async_copy(qkv_ref.at[device], qkv_hbm.at[device], out_sems.at[0, device])
        )
        departures[-1].start()
    for arrival in arrivals[3]:
        arrival.wait()
    for device in range(devices):
        by_device_ref[device] = cot_ref[:, device * width : (device + 1) * width]
        departures.append(
            pltpu.make_async_copy(
                by_device_ref.at[device], by_device_hbm.at[device], out_sems.at[1, device]
            )
        )
        departures[-1].start()
    for departure in departures:
        departure.wait()


def by_device(queries, key_vectors, value_vectors, grad_out, devices):
    tokens = queries.shape[0]
    width = queries.shape[1] // devices
    outs = (
        jax.ShapeDtypeStruct((devices, tokens, width + 2 * FEAT), jnp.bfloat16),
        jax.ShapeDtypeStruct((devices, tokens, width), jnp.bfloat16),
    )
    arrays = (queries, key_vectors, value_vectors, grad_out, *outs)
    return pl.pallas_call(
        functools.partial(prologue_kernel, devices // KV_HEADS),
        out_shape=outs,
        in_specs=[ANY] * 4,
        out_specs=(ANY, ANY),
        scratch_shapes=[pltpu.VMEM(array.shape, array.dtype) for array in arrays]
        + [pltpu.SemaphoreType.DMA((4, 4)), pltpu.SemaphoreType.DMA((2, devices))],
        compiler_params=LARGE,
    )(queries, key_vectors, value_vectors, grad_out)


def epilogue_kernel(repeats, grads_ref, attn_ref, out_ref, dq_ref, dk_ref, dv_ref):
    devices, _, width = attn_ref.shape
    for device in range(devices):
        cols = slice(device * width, (device + 1) * width)
        out_ref[:, cols] = attn_ref[device]
        dq_ref[:, cols] = grads_ref[device, :, :width]
    for head in range(devices // repeats):
        cols = slice(head * FEAT, (head + 1) * FEAT)
        for ref, at in ((dk_ref, width), (dv_ref, width + FEAT)):
            parts = [
                grads_ref[head * repeats + part, :, at : at + FEAT].astype(jnp.float32)
                for part in range(repeats)
            ]
            ref[:, cols] = functools.reduce(jnp.add, parts).astype(jnp.bfloat16)


def by_token(grads, attn):
    devices, tokens, width = attn.shape
    wide = jax.ShapeDtypeStruct((tokens, devices * width), jnp.bfloat16)
    narrow = jax.ShapeDtypeStruct((tokens, KV_HEADS * FEAT), jnp.bfloat16)
    return pl.pallas_call(
        functools.partial(epilogue_kernel, devices // KV_HEADS),
        out_shape=(wide, wide, narrow, narrow),
        in_specs=[VMEM] * 2,
        out_specs=(VMEM,) * 4,
        compiler_params=SMALL,
    )(grads, attn)


def over_heads(block):
    return lax.all_to_all(block, "head", split_axis=0, concat_axis=0, tiled=True)


def hop(block, distance):
    count = lax.axis_size("grp")
    return lax.ppermute(block, "grp", [(i, (i + distance) % count) for i in range(count)])


LONG_WAY = {5: 4, 6: 5}


def along_rows(block, distance, split=False):
    count = lax.axis_size("grp")
    distance %= count
    short = distance if 2 * distance <= count else distance - count
    parts = LONG_WAY.get(abs(short), 0) * block.shape[0] // 16
    if not parts or not split:
        return hop(block, short)
    long = short - count if short > 0 else short + count
    far = hop(block[:parts], long // 2)
    near = hop(block[parts:], short)
    far = hop(far, long - long // 2)
    return jnp.concatenate([far, near], axis=0)


def first_part(shift, cotangent):
    return along_rows(cotangent, -shift)


def last_part(shift, attn):
    return along_rows(attn, shift, split=True)


def shards(queries, key_vectors, value_vectors, grad_out, doc_lengths, parcel_shift):
    group = lax.axis_index("grp").astype(jnp.int32).reshape(1)
    devices = lax.axis_size("head")
    heads = HEADS // devices
    shifts = range(1, lax.axis_size("grp"))
    choice = parcel_shift[0] - 1

    qkv, cotangent = by_device(queries, key_vectors, value_vectors, grad_out, devices)
    shape = cotangent.shape
    qkv = over_heads(qkv)
    cotangent = lax.switch(choice, [functools.partial(first_part, s) for s in shifts], cotangent)
    qkv, cotangent = lax.optimization_barrier((qkv, cotangent))
    qkv = qkv.reshape(shape[0] * shape[1], -1)
    cotangent = over_heads(cotangent)
    output, marks = attend(group, doc_lengths, qkv, heads)
    attn, cotangent = lax.optimization_barrier((output.reshape(shape), cotangent))
    attn = over_heads(attn)
    cotangent = cotangent.reshape(output.shape)
    grads = attend_back(group, doc_lengths, qkv, output, marks, cotangent, heads)
    grads = grads.reshape(shape[0], shape[1], -1)
    grads, attn = lax.optimization_barrier((grads, attn))
    grads = over_heads(grads)
    attn = lax.switch(choice, [functools.partial(last_part, s) for s in shifts], attn)
    return by_token(grads, attn)


def solution(mesh):
    split = P(("grp", "head"), None)
    return jax.shard_map(
        shards,
        mesh=mesh,
        in_specs=(split, split, split, split, P(), P()),
        out_specs=(split, split, split, split),
        check_vma=False,
    )
```

```python
import functools
import math

import jax
import jax.numpy as jnp
from jax import lax
from jax.experimental import pallas as pl
from jax.experimental.pallas import tpu as pltpu
from jax.sharding import PartitionSpec as P

HEADS = 32
KV_HEADS = 8
FEAT = 128
DOCS = 3
BLOCK = 512
SCALING = FEAT**-0.5
LOG2_SCALING = SCALING * math.log2(math.e)
EXCLUDED = -1e30


def dot(a, b):
    return jnp.dot(a, b, preferred_element_type=jnp.float32)


def rows(block):
    return pl.ds(pl.multiple_of(block * BLOCK, BLOCK), BLOCK)


def start_of(position, first, second):
    return jnp.where(position < first, 0, jnp.where(position < second, first, second))


def lanes_and_documents(block, first, second):
    lane = lax.broadcasted_iota(jnp.int32, (BLOCK, FEAT), 1)
    position = block * BLOCK + lax.broadcasted_iota(jnp.int32, (BLOCK, FEAT), 0)
    return lane, (position >= first).astype(jnp.int32) + (position >= second).astype(jnp.int32)


def in_lanes(lane, column):
    high = column.astype(jnp.bfloat16).astype(jnp.float32)
    middle = (column - high).astype(jnp.bfloat16).astype(jnp.float32)
    low = column - high - middle
    picked = jnp.where(lane == DOCS, high, jnp.where(lane == DOCS + 1, middle, low))
    return jnp.where((lane >= DOCS) & (lane < DOCS + 3), picked, 0.0)


def fill_key_marks(marks_ref, block, first, second):
    lane, document = lanes_and_documents(block, first, second)
    marked = (lane == document) | ((lane >= DOCS) & (lane < DOCS + 3))
    marks_ref[rows(block), :] = marked.astype(jnp.float32).astype(jnp.bfloat16)


def causal_rows(values):
    query = lax.rem(lax.broadcasted_iota(jnp.int32, values.shape, 0), BLOCK)
    key = lax.broadcasted_iota(jnp.int32, values.shape, 1)
    return jnp.where(key <= query, values, EXCLUDED)


def folded(combine, values):
    parts = [values[:, at : at + FEAT] for at in range(0, values.shape[1], FEAT)]
    return functools.reduce(combine, parts)


def forward_kernel(
    heads,
    group_ref,
    lengths_ref,
    qkv_hbm,
    out_hbm,
    marks_hbm,
    qkv_ref,
    out_ref,
    marks_ref,
    kt_ref,
    query_ref,
    scores_ref,
    top_ref,
    total_ref,
    acc_ref,
    in_sems,
    out_sems,
):
    blocks = qkv_ref.shape[0] // BLOCK
    group = group_ref[0]
    first = lengths_ref[group, 0]
    second = first + lengths_ref[group, 1]
    key_cols = slice(heads * FEAT, (heads + 1) * FEAT)
    value_cols = slice((heads + 1) * FEAT, (heads + 2) * FEAT)

    def arrival(block):
        here = rows(block)
        return pltpu.make_async_copy(qkv_hbm.at[here, :], qkv_ref.at[here, :], in_sems.at[block])

    def departures(block):
        here = rows(block)
        return (
            pltpu.make_async_copy(out_ref.at[here, :], out_hbm.at[here, :], out_sems.at[0, block]),
            pltpu.make_async_copy(
                marks_ref.at[here, :], marks_hbm.at[here, :], out_sems.at[1, block]
            ),
        )

    for block in range(blocks):
        arrival(block).start()

    def one_query_block(block, _):
        arrival(block).wait()
        kt_ref[block, :FEAT, :] = qkv_ref[rows(block), key_cols].T
        kind = lax.broadcasted_iota(jnp.int32, (FEAT, BLOCK), 0)
        position = block * BLOCK + lax.broadcasted_iota(jnp.int32, (FEAT, BLOCK), 1)
        document = (position >= first).astype(jnp.int32) + (position >= second).astype(jnp.int32)
        kt_ref[block, FEAT:, :] = (kind == document).astype(jnp.float32).astype(jnp.bfloat16)
        lane, document = lanes_and_documents(block, first, second)
        marks = jnp.where((lane != document) & (lane < DOCS), EXCLUDED, 0.0)
        for h in range(heads):
            query_ref[h * BLOCK : (h + 1) * BLOCK, :FEAT] = qkv_ref[
                rows(block), h * FEAT : (h + 1) * FEAT
            ]
            query_ref[h * BLOCK : (h + 1) * BLOCK, FEAT:] = marks.astype(jnp.bfloat16)
        lowest = start_of(block * BLOCK, first, second) // BLOCK
        scores = causal_rows(dot(query_ref[...], kt_ref[block]))
        scores_ref[block] = scores
        top_ref[...] = folded(jnp.maximum, scores)

        def earlier(key_block, _):
            scores = dot(query_ref[...], kt_ref[key_block])
            scores_ref[key_block] = scores
            top_ref[...] = jnp.maximum(top_ref[...], folded(jnp.maximum, scores))
            return 0

        lax.fori_loop(lowest, block, earlier, 0)
        top = jnp.max(top_ref[...], axis=1, keepdims=True) * LOG2_SCALING
        top_ref[...] = jnp.broadcast_to(top, top_ref.shape)
        total_ref[...] = jnp.zeros_like(total_ref)
        acc_ref[...] = jnp.zeros_like(acc_ref)

        def weigh(key_block, _):
            top = top_ref[...]
            exponent = jnp.exp2(
                scores_ref[key_block] * LOG2_SCALING - jnp.concatenate([top] * (BLOCK // FEAT), axis=1)
            )
            total_ref[...] += folded(jnp.add, exponent)
            acc_ref[...] += dot(exponent.astype(jnp.bfloat16), qkv_ref[rows(key_block), value_cols])
            return 0

        lax.fori_loop(lowest, block + 1, weigh, 0)
        total = jnp.sum(total_ref[...], axis=1, keepdims=True)
        output = (acc_ref[...] * (1.0 / total)).astype(jnp.bfloat16)
        lse = (top + jnp.log2(total)) * (-1.0 / LOG2_SCALING)
        for h in range(heads):
            here = slice(h * BLOCK, (h + 1) * BLOCK)
            out_ref[rows(block), h * FEAT : (h + 1) * FEAT] = output[here]
            marks_ref[rows(block), h * FEAT : (h + 1) * FEAT] = (
                marks + in_lanes(lane, lse[here])
            ).astype(jnp.bfloat16)
        for departure in departures(block):
            departure.start()
        return 0

    lax.fori_loop(0, blocks, one_query_block, 0)
    for block in range(blocks):
        for departure in departures(block):
            departure.wait()


def backward_kernel(
    heads,
    group_ref,
    lengths_ref,
    qkv_hbm,
    out_hbm,
    marks_hbm,
    cot_hbm,
    grad_hbm,
    qkv_ref,
    out_ref,
    marks_ref,
    cot_ref,
    grad_ref,
    key_marks_ref,
    kt_ref,
    query_ref,
    cotangent_ref,
    query_t_ref,
    cotangent_t_ref,
    dq_ref,
    dk_ref,
    dv_ref,
    in_sems,
    out_sems,
):
    blocks = qkv_ref.shape[0] // BLOCK
    group = group_ref[0]
    first = lengths_ref[group, 0]
    second = first + lengths_ref[group, 1]
    query_cols = slice(0, heads * FEAT)
    key_cols = slice(heads * FEAT, (heads + 1) * FEAT)
    value_cols = slice((heads + 1) * FEAT, (heads + 2) * FEAT)
    shared_cols = slice(heads * FEAT, (heads + 2) * FEAT)

    def arrivals(block):
        here = rows(block)
        pairs = ((qkv_hbm, qkv_ref), (out_hbm, out_ref), (marks_hbm, marks_ref), (cot_hbm, cot_ref))
        return [
            pltpu.make_async_copy(source.at[here, :], target.at[here, :], in_sems.at[n, block])
            for n, (source, target) in enumerate(pairs)
        ]

    def departure(block, cols, which):
        here = rows(block)
        return pltpu.make_async_copy(
            grad_ref.at[here, cols], grad_hbm.at[here, cols], out_sems.at[which, block]
        )

    for block in range(blocks):
        for arrival in arrivals(block):
            arrival.start()

    half = BLOCK // 2
    columns = heads * half

    def one_query_block(block, _):
        for arrival in arrivals(block):
            arrival.wait()
        fill_key_marks(key_marks_ref, block, first, second)
        kt_ref[block] = qkv_ref[rows(block), key_cols].T
        dk_ref[rows(block), :] = jnp.zeros((BLOCK, FEAT), jnp.float32)
        dv_ref[rows(block), :] = jnp.zeros((BLOCK, FEAT), jnp.float32)
        lane = lax.broadcasted_iota(jnp.int32, (half, FEAT), 1)
        places = []
        for part in range(2):
            for h in range(heads):
                at = (part * heads + h) * half
                here = pl.ds(pl.multiple_of(block * BLOCK + part * half, half), half)
                places.append((slice(at, at + half), here, slice(h * FEAT, (h + 1) * FEAT)))
        for at, here, cols in places:
            query_ref[at, :FEAT] = qkv_ref[here, cols]
            query_ref[at, FEAT:] = marks_ref[here, cols]
            cotangent = cot_ref[here, cols]
            product = cotangent.astype(jnp.float32) * out_ref[here, cols].astype(jnp.float32)
            delta = jnp.sum(product, axis=1, keepdims=True)
            cotangent_ref[at, :FEAT] = cotangent
            cotangent_ref[at, FEAT:] = in_lanes(lane, -delta).astype(jnp.bfloat16)
        query_t_ref[...] = query_ref[...].T
        cotangent_t_ref[...] = cotangent_ref[...].T
        dq_ref[...] = jnp.zeros_like(dq_ref)

        def add_part(key_block, keys_at, cols, diagonal):
            begin = pl.multiple_of(key_block * BLOCK + keys_at.start, half)
            here = pl.ds(begin, keys_at.stop - keys_at.start)
            key_marks = key_marks_ref[here, :]
            keys = jnp.concatenate([qkv_ref[here, key_cols], key_marks], axis=1)
            values = jnp.concatenate([qkv_ref[here, value_cols], key_marks], axis=1)
            probs = jnp.exp2(dot(keys, query_t_ref[:, cols]) * LOG2_SCALING)
            if diagonal:
                key = keys_at.start + lax.broadcasted_iota(jnp.int32, probs.shape, 0)
                column = cols.start + lax.broadcasted_iota(jnp.int32, probs.shape, 1)
                query = jnp.where(column < columns, 0, half) + lax.rem(column, half)
                probs = jnp.where(key <= query, probs, 0.0)
            grad_score = probs * dot(values, cotangent_t_ref[:, cols])
            grad_score = grad_score.astype(jnp.bfloat16)
            dv_ref[here, :] += dot(probs.astype(jnp.bfloat16), cotangent_ref[cols, :FEAT])
            dk_ref[here, :] += dot(grad_score, query_ref[cols, :FEAT])
            dq_ref[:, cols] += dot(kt_ref[key_block, :, keys_at], grad_score)

        def for_first_half(key_block, _):
            add_part(key_block, slice(0, BLOCK), slice(0, columns), False)
            return 0

        def for_both(key_block, _):
            add_part(key_block, slice(0, BLOCK), slice(0, 2 * columns), False)
            return 0

        lowest = start_of(block * BLOCK, first, second) // BLOCK
        lowest_of_both = start_of(block * BLOCK + half, first, second) // BLOCK
        lax.fori_loop(lowest, lowest_of_both, for_first_half, 0)
        lax.fori_loop(lowest_of_both, block, for_both, 0)
        add_part(block, slice(0, half), slice(0, 2 * columns), True)
        add_part(block, slice(half, BLOCK), slice(columns, 2 * columns), True)
        dq = (dq_ref[...] * SCALING).T.astype(jnp.bfloat16)
        for at, here, cols in places:
            grad_ref[here, cols] = dq[at]
        departure(block, query_cols, 0).start()
        return 0

    lax.fori_loop(0, blocks, one_query_block, 0)

    def finish(block, _):
        grad_ref[rows(block), key_cols] = (dk_ref[rows(block), :] * SCALING).astype(jnp.bfloat16)
        grad_ref[rows(block), value_cols] = dv_ref[rows(block), :].astype(jnp.bfloat16)
        departure(block, shared_cols, 1).start()
        return 0

    lax.fori_loop(0, blocks, finish, 0)
    for block in range(blocks):
        departure(block, query_cols, 0).wait()
        departure(block, shared_cols, 1).wait()


SMEM = pl.BlockSpec(memory_space=pltpu.SMEM)
VMEM = pl.BlockSpec(memory_space=pltpu.VMEM)
ANY = pl.BlockSpec(memory_space=pl.ANY)
SMALL = pltpu.CompilerParams(vmem_limit_bytes=32 * 2**20)
LARGE = pltpu.CompilerParams(vmem_limit_bytes=56 * 2**20)


def attend(group, doc_lengths, qkv, heads):
    tokens = qkv.shape[0]
    blocks = tokens // BLOCK
    columns = heads * BLOCK
    wide = jax.ShapeDtypeStruct((tokens, heads * FEAT), jnp.bfloat16)
    return pl.pallas_call(
        functools.partial(forward_kernel, heads),
        out_shape=(wide, wide),
        in_specs=[SMEM, SMEM, ANY],
        out_specs=(ANY, ANY),
        scratch_shapes=[
            pltpu.VMEM(qkv.shape, jnp.bfloat16),
            pltpu.VMEM(wide.shape, jnp.bfloat16),
            pltpu.VMEM(wide.shape, jnp.bfloat16),
            pltpu.VMEM((blocks, 2 * FEAT, BLOCK), jnp.bfloat16),
            pltpu.VMEM((columns, 2 * FEAT), jnp.bfloat16),
            pltpu.VMEM((blocks, columns, BLOCK), jnp.float32),
            pltpu.VMEM((columns, FEAT), jnp.float32),
            pltpu.VMEM((columns, FEAT), jnp.float32),
            pltpu.VMEM((columns, FEAT), jnp.float32),
            pltpu.SemaphoreType.DMA((blocks,)),
            pltpu.SemaphoreType.DMA((2, blocks)),
        ],
        compiler_params=LARGE,
        cost_estimate=pl.CostEstimate(
            flops=2 * 2 * heads * tokens * tokens * FEAT,
            bytes_accessed=4 * 2**20,
            transcendentals=heads * tokens * tokens // 2,
        ),
    )(group, doc_lengths, qkv)


def attend_back(group, doc_lengths, qkv, output, marks, cotangent, heads):
    tokens = qkv.shape[0]
    blocks = tokens // BLOCK
    columns = heads * BLOCK
    return pl.pallas_call(
        functools.partial(backward_kernel, heads),
        out_shape=jax.ShapeDtypeStruct(qkv.shape, jnp.bfloat16),
        in_specs=[SMEM, SMEM, ANY, ANY, ANY, ANY],
        out_specs=ANY,
        scratch_shapes=[
            pltpu.VMEM(qkv.shape, jnp.bfloat16),
            pltpu.VMEM(output.shape, jnp.bfloat16),
            pltpu.VMEM(marks.shape, jnp.bfloat16),
            pltpu.VMEM(cotangent.shape, jnp.bfloat16),
            pltpu.VMEM(qkv.shape, jnp.bfloat16),
            pltpu.VMEM((tokens, FEAT), jnp.bfloat16),
            pltpu.VMEM((blocks, FEAT, BLOCK), jnp.bfloat16),
            pltpu.VMEM((columns, 2 * FEAT), jnp.bfloat16),
            pltpu.VMEM((columns, 2 * FEAT), jnp.bfloat16),
            pltpu.VMEM((2 * FEAT, columns), jnp.bfloat16),
            pltpu.VMEM((2 * FEAT, columns), jnp.bfloat16),
            pltpu.VMEM((FEAT, columns), jnp.float32),
            pltpu.VMEM((tokens, FEAT), jnp.float32),
            pltpu.VMEM((tokens, FEAT), jnp.float32),
            pltpu.SemaphoreType.DMA((4, blocks)),
            pltpu.SemaphoreType.DMA((2, blocks)),
        ],
        compiler_params=LARGE,
        cost_estimate=pl.CostEstimate(
            flops=5 * 2 * heads * tokens * tokens * FEAT,
            bytes_accessed=7 * 2**20,
            transcendentals=heads * tokens * tokens // 2,
        ),
    )(group, doc_lengths, qkv, output, marks, cotangent)


def prologue_kernel(
    repeats,
    q_hbm,
    k_hbm,
    v_hbm,
    cot_hbm,
    qkv_hbm,
    by_device_hbm,
    q_ref,
    k_ref,
    v_ref,
    cot_ref,
    qkv_ref,
    by_device_ref,
    in_sems,
    out_sems,
):
    devices, tokens, width = by_device_hbm.shape
    parts = in_sems.shape[1]
    span = tokens // parts
    arrivals = [
        [
            pltpu.make_async_copy(
                source.at[part * span : (part + 1) * span, :],
                target.at[part * span : (part + 1) * span, :],
                in_sems.at[n, part],
            )
            for part in range(parts)
        ]
        for n, (source, target) in enumerate(
            ((q_hbm, q_ref), (k_hbm, k_ref), (v_hbm, v_ref), (cot_hbm, cot_ref))
        )
    ]
    for group in arrivals:
        for arrival in group:
            arrival.start()
    for group in arrivals[:3]:
        for arrival in group:
            arrival.wait()
    departures = []
    for device in range(devices):
        shared = slice(device // repeats * FEAT, (device // repeats + 1) * FEAT)
        qkv_ref[device, :, :width] = q_ref[:, device * width : (device + 1) * width]
        qkv_ref[device, :, width : width + FEAT] = k_ref[:, shared]
        qkv_ref[device, :, width + FEAT :] = v_ref[:, shared]
        departures.append(
            pltpu.make_async_copy(qkv_ref.at[device], qkv_hbm.at[device], out_sems.at[0, device])
        )
        departures[-1].start()
    for arrival in arrivals[3]:
        arrival.wait()
    for device in range(devices):
        by_device_ref[device] = cot_ref[:, device * width : (device + 1) * width]
        departures.append(
            pltpu.make_async_copy(
                by_device_ref.at[device], by_device_hbm.at[device], out_sems.at[1, device]
            )
        )
        departures[-1].start()
    for departure in departures:
        departure.wait()


def by_device(queries, key_vectors, value_vectors, grad_out, devices):
    tokens = queries.shape[0]
    width = queries.shape[1] // devices
    outs = (
        jax.ShapeDtypeStruct((devices, tokens, width + 2 * FEAT), jnp.bfloat16),
        jax.ShapeDtypeStruct((devices, tokens, width), jnp.bfloat16),
    )
    arrays = (queries, key_vectors, value_vectors, grad_out, *outs)
    return pl.pallas_call(
        functools.partial(prologue_kernel, devices // KV_HEADS),
        out_shape=outs,
        in_specs=[ANY] * 4,
        out_specs=(ANY, ANY),
        scratch_shapes=[pltpu.VMEM(array.shape, array.dtype) for array in arrays]
        + [pltpu.SemaphoreType.DMA((4, 4)), pltpu.SemaphoreType.DMA((2, devices))],
        compiler_params=LARGE,
    )(queries, key_vectors, value_vectors, grad_out)


def epilogue_kernel(
    repeats,
    grads_ref,
    attn_ref,
    out_hbm,
    dq_hbm,
    dk_hbm,
    dv_hbm,
    out_ref,
    dq_ref,
    dk_ref,
    dv_ref,
    sems,
):
    devices, tokens, width = attn_ref.shape
    parts = sems.shape[1]
    span = tokens // parts

    def departures(part):
        here = pl.ds(pl.multiple_of(part * span, span), span)
        pairs = ((out_ref, out_hbm), (dq_ref, dq_hbm), (dk_ref, dk_hbm), (dv_ref, dv_hbm))
        return [
            pltpu.make_async_copy(source.at[here, :], target.at[here, :], sems.at[n, part])
            for n, (source, target) in enumerate(pairs)
        ]

    def lay_out(part, _):
        here = pl.ds(pl.multiple_of(part * span, span), span)
        for device in range(devices):
            cols = slice(device * width, (device + 1) * width)
            out_ref[here, cols] = attn_ref[device, here, :]
            dq_ref[here, cols] = grads_ref[device, here, :width]
        for head in range(devices // repeats):
            cols = slice(head * FEAT, (head + 1) * FEAT)
            for ref, at in ((dk_ref, width), (dv_ref, width + FEAT)):
                terms = [
                    grads_ref[head * repeats + n, here, at : at + FEAT].astype(jnp.float32)
                    for n in range(repeats)
                ]
                ref[here, cols] = functools.reduce(jnp.add, terms).astype(jnp.bfloat16)
        for departure in departures(part):
            departure.start()
        return 0

    def finish(part, _):
        for departure in departures(part):
            departure.wait()
        return 0

    lax.fori_loop(0, parts, lay_out, 0)
    lax.fori_loop(0, parts, finish, 0)


def by_token(grads, attn):
    devices, tokens, width = attn.shape
    wide = jax.ShapeDtypeStruct((tokens, devices * width), jnp.bfloat16)
    narrow = jax.ShapeDtypeStruct((tokens, KV_HEADS * FEAT), jnp.bfloat16)
    outs = (wide, wide, narrow, narrow)
    return pl.pallas_call(
        functools.partial(epilogue_kernel, devices // KV_HEADS),
        out_shape=outs,
        in_specs=[VMEM] * 2,
        out_specs=(ANY,) * 4,
        scratch_shapes=[pltpu.VMEM(out.shape, out.dtype) for out in outs]
        + [pltpu.SemaphoreType.DMA((4, 4))],
        compiler_params=SMALL,
    )(grads, attn)


def over_heads(block):
    return lax.all_to_all(block, "head", split_axis=0, concat_axis=0, tiled=True)


def hop(block, distance):
    count = lax.axis_size("grp")
    return lax.ppermute(block, "grp", [(i, (i + distance) % count) for i in range(count)])


LONG_WAY = {5: 4, 6: 5}


def along_rows(block, distance, split=False):
    count = lax.axis_size("grp")
    distance %= count
    short = distance if 2 * distance <= count else distance - count
    parts = LONG_WAY.get(abs(short), 0) * block.shape[0] // 16
    if not parts or not split:
        return hop(block, short)
    long = short - count if short > 0 else short + count
    far = hop(block[:parts], long // 2)
    near = hop(block[parts:], short)
    far = hop(far, long - long // 2)
    return jnp.concatenate([far, near], axis=0)


def first_part(shift, cotangent):
    return along_rows(cotangent, -shift)


def last_part(shift, attn):
    return along_rows(attn, shift, split=True)


def shards(queries, key_vectors, value_vectors, grad_out, doc_lengths, parcel_shift):
    group = lax.axis_index("grp").astype(jnp.int32).reshape(1)
    devices = lax.axis_size("head")
    heads = HEADS // devices
    shifts = range(1, lax.axis_size("grp"))
    choice = parcel_shift[0] - 1

    qkv, cotangent = by_device(queries, key_vectors, value_vectors, grad_out, devices)
    shape = cotangent.shape
    qkv = over_heads(qkv)
    cotangent = lax.switch(choice, [functools.partial(first_part, s) for s in shifts], cotangent)
    qkv, cotangent = lax.optimization_barrier((qkv, cotangent))
    qkv = qkv.reshape(shape[0] * shape[1], -1)
    cotangent = over_heads(cotangent)
    output, marks = attend(group, doc_lengths, qkv, heads)
    attn, cotangent = lax.optimization_barrier((output.reshape(shape), cotangent))
    attn = over_heads(attn)
    cotangent = cotangent.reshape(output.shape)
    grads = attend_back(group, doc_lengths, qkv, output, marks, cotangent, heads)
    grads = grads.reshape(shape[0], shape[1], -1)
    grads, attn = lax.optimization_barrier((grads, attn))
    grads = over_heads(grads)
    attn = lax.switch(choice, [functools.partial(last_part, s) for s in shifts], attn)
    return by_token(grads, attn)


def solution(mesh):
    split = P(("grp", "head"), None)
    return jax.shard_map(
        shards,
        mesh=mesh,
        in_specs=(split, split, split, split, P(), P()),
        out_specs=(split, split, split, split),
        check_vma=False,
    )
```

```python
import functools
import math

import jax
import jax.numpy as jnp
from jax import lax
from jax.experimental import pallas as pl
from jax.experimental.pallas import tpu as pltpu
from jax.sharding import PartitionSpec as P

HEADS = 32
KV_HEADS = 8
FEAT = 128
DOCS = 3
BLOCK = 512
SCALING = FEAT**-0.5
LOG2_SCALING = SCALING * math.log2(math.e)
EXCLUDED = -1e30


def dot(a, b):
    return jnp.dot(a, b, preferred_element_type=jnp.float32)


def rows(block):
    return pl.ds(pl.multiple_of(block * BLOCK, BLOCK), BLOCK)


def start_of(position, first, second):
    return jnp.where(position < first, 0, jnp.where(position < second, first, second))


def lanes_and_documents(block, first, second):
    lane = lax.broadcasted_iota(jnp.int32, (BLOCK, FEAT), 1)
    position = block * BLOCK + lax.broadcasted_iota(jnp.int32, (BLOCK, FEAT), 0)
    return lane, (position >= first).astype(jnp.int32) + (position >= second).astype(jnp.int32)


def in_lanes(lane, column):
    high = column.astype(jnp.bfloat16).astype(jnp.float32)
    middle = (column - high).astype(jnp.bfloat16).astype(jnp.float32)
    low = column - high - middle
    picked = jnp.where(lane == DOCS, high, jnp.where(lane == DOCS + 1, middle, low))
    return jnp.where((lane >= DOCS) & (lane < DOCS + 3), picked, 0.0)


def fill_key_marks(marks_ref, block, first, second):
    lane, document = lanes_and_documents(block, first, second)
    marked = (lane == document) | ((lane >= DOCS) & (lane < DOCS + 3))
    marks_ref[rows(block), :] = marked.astype(jnp.float32).astype(jnp.bfloat16)


def causal_rows(values):
    query = lax.rem(lax.broadcasted_iota(jnp.int32, values.shape, 0), BLOCK)
    key = lax.broadcasted_iota(jnp.int32, values.shape, 1)
    return jnp.where(key <= query, values, EXCLUDED)


def folded(combine, values):
    parts = [values[:, at : at + FEAT] for at in range(0, values.shape[1], FEAT)]
    return functools.reduce(combine, parts)


def forward_kernel(
    heads,
    group_ref,
    lengths_ref,
    qkv_hbm,
    out_hbm,
    marks_hbm,
    qkv_ref,
    out_ref,
    marks_ref,
    kt_ref,
    query_ref,
    scores_ref,
    top_ref,
    total_ref,
    acc_ref,
    in_sems,
    out_sems,
):
    blocks = qkv_ref.shape[0] // BLOCK
    group = group_ref[0]
    first = lengths_ref[0, group]
    second = first + lengths_ref[1, group]
    key_cols = slice(heads * FEAT, (heads + 1) * FEAT)
    value_cols = slice((heads + 1) * FEAT, (heads + 2) * FEAT)

    def arrival(block):
        here = rows(block)
        return pltpu.make_async_copy(qkv_hbm.at[here, :], qkv_ref.at[here, :], in_sems.at[block])

    def departures(block):
        here = rows(block)
        return (
            pltpu.make_async_copy(out_ref.at[here, :], out_hbm.at[here, :], out_sems.at[0, block]),
            pltpu.make_async_copy(
                marks_ref.at[here, :], marks_hbm.at[here, :], out_sems.at[1, block]
            ),
        )

    for block in range(blocks):
        arrival(block).start()

    def one_query_block(block, _):
        arrival(block).wait()
        kt_ref[block, :FEAT, :] = qkv_ref[rows(block), key_cols].T
        kind = lax.broadcasted_iota(jnp.int32, (FEAT, BLOCK), 0)
        position = block * BLOCK + lax.broadcasted_iota(jnp.int32, (FEAT, BLOCK), 1)
        document = (position >= first).astype(jnp.int32) + (position >= second).astype(jnp.int32)
        kt_ref[block, FEAT:, :] = (kind == document).astype(jnp.float32).astype(jnp.bfloat16)
        lane, document = lanes_and_documents(block, first, second)
        marks = jnp.where((lane != document) & (lane < DOCS), EXCLUDED, 0.0)
        for h in range(heads):
            query_ref[h * BLOCK : (h + 1) * BLOCK, :FEAT] = qkv_ref[
                rows(block), h * FEAT : (h + 1) * FEAT
            ]
            query_ref[h * BLOCK : (h + 1) * BLOCK, FEAT:] = marks.astype(jnp.bfloat16)
        lowest = start_of(block * BLOCK, first, second) // BLOCK
        scores = causal_rows(dot(query_ref[...], kt_ref[block]))
        scores_ref[block] = scores
        top_ref[...] = folded(jnp.maximum, scores)

        def earlier(key_block, _):
            scores = dot(query_ref[...], kt_ref[key_block])
            scores_ref[key_block] = scores
            top_ref[...] = jnp.maximum(top_ref[...], folded(jnp.maximum, scores))
            return 0

        lax.fori_loop(lowest, block, earlier, 0)
        top = jnp.max(top_ref[...], axis=1, keepdims=True) * LOG2_SCALING
        top_ref[...] = jnp.broadcast_to(top, top_ref.shape)
        total_ref[...] = jnp.zeros_like(total_ref)
        acc_ref[...] = jnp.zeros_like(acc_ref)

        def weigh(key_block, _):
            top = top_ref[...]
            exponent = jnp.exp2(
                scores_ref[key_block] * LOG2_SCALING - jnp.concatenate([top] * (BLOCK // FEAT), axis=1)
            )
            total_ref[...] += folded(jnp.add, exponent)
            acc_ref[...] += dot(exponent.astype(jnp.bfloat16), qkv_ref[rows(key_block), value_cols])
            return 0

        lax.fori_loop(lowest, block + 1, weigh, 0)
        total = jnp.sum(total_ref[...], axis=1, keepdims=True)
        output = (acc_ref[...] * (1.0 / total)).astype(jnp.bfloat16)
        lse = (top + jnp.log2(total)) * (-1.0 / LOG2_SCALING)
        for h in range(heads):
            here = slice(h * BLOCK, (h + 1) * BLOCK)
            out_ref[rows(block), h * FEAT : (h + 1) * FEAT] = output[here]
            marks_ref[rows(block), h * FEAT : (h + 1) * FEAT] = (
                marks + in_lanes(lane, lse[here])
            ).astype(jnp.bfloat16)
        for departure in departures(block):
            departure.start()
        return 0

    lax.fori_loop(0, blocks, one_query_block, 0)
    for block in range(blocks):
        for departure in departures(block):
            departure.wait()


def backward_kernel(
    heads,
    group_ref,
    lengths_ref,
    qkv_hbm,
    out_hbm,
    marks_hbm,
    cot_hbm,
    grad_hbm,
    qkv_ref,
    out_ref,
    marks_ref,
    cot_ref,
    grad_ref,
    key_marks_ref,
    kt_ref,
    query_ref,
    cotangent_ref,
    query_t_ref,
    cotangent_t_ref,
    dq_ref,
    dk_ref,
    dv_ref,
    in_sems,
    out_sems,
):
    blocks = qkv_ref.shape[0] // BLOCK
    group = group_ref[0]
    first = lengths_ref[0, group]
    second = first + lengths_ref[1, group]
    query_cols = slice(0, heads * FEAT)
    key_cols = slice(heads * FEAT, (heads + 1) * FEAT)
    value_cols = slice((heads + 1) * FEAT, (heads + 2) * FEAT)
    shared_cols = slice(heads * FEAT, (heads + 2) * FEAT)

    def arrivals(block):
        here = rows(block)
        pairs = ((qkv_hbm, qkv_ref), (out_hbm, out_ref), (marks_hbm, marks_ref), (cot_hbm, cot_ref))
        return [
            pltpu.make_async_copy(source.at[here, :], target.at[here, :], in_sems.at[n, block])
            for n, (source, target) in enumerate(pairs)
        ]

    def departure(block, cols, which):
        here = rows(block)
        return pltpu.make_async_copy(
            grad_ref.at[here, cols], grad_hbm.at[here, cols], out_sems.at[which, block]
        )

    for block in range(blocks):
        for arrival in arrivals(block):
            arrival.start()

    half = BLOCK // 2
    columns = heads * half

    def one_query_block(block, _):
        for arrival in arrivals(block):
            arrival.wait()
        fill_key_marks(key_marks_ref, block, first, second)
        kt_ref[block] = qkv_ref[rows(block), key_cols].T
        dk_ref[rows(block), :] = jnp.zeros((BLOCK, FEAT), jnp.float32)
        dv_ref[rows(block), :] = jnp.zeros((BLOCK, FEAT), jnp.float32)
        lane = lax.broadcasted_iota(jnp.int32, (half, FEAT), 1)
        places = []
        for part in range(2):
            for h in range(heads):
                at = (part * heads + h) * half
                here = pl.ds(pl.multiple_of(block * BLOCK + part * half, half), half)
                places.append((slice(at, at + half), here, slice(h * FEAT, (h + 1) * FEAT)))
        for at, here, cols in places:
            query_ref[at, :FEAT] = qkv_ref[here, cols]
            query_ref[at, FEAT:] = marks_ref[here, cols]
            cotangent = cot_ref[here, cols]
            product = cotangent.astype(jnp.float32) * out_ref[here, cols].astype(jnp.float32)
            delta = jnp.sum(product, axis=1, keepdims=True)
            cotangent_ref[at, :FEAT] = cotangent
            cotangent_ref[at, FEAT:] = in_lanes(lane, -delta).astype(jnp.bfloat16)
        query_t_ref[...] = query_ref[...].T
        cotangent_t_ref[...] = cotangent_ref[...].T
        dq_ref[...] = jnp.zeros_like(dq_ref)

        def add_part(key_block, keys_at, cols, diagonal):
            begin = pl.multiple_of(key_block * BLOCK + keys_at.start, half)
            here = pl.ds(begin, keys_at.stop - keys_at.start)
            key_marks = key_marks_ref[here, :]
            keys = jnp.concatenate([qkv_ref[here, key_cols], key_marks], axis=1)
            values = jnp.concatenate([qkv_ref[here, value_cols], key_marks], axis=1)
            probs = jnp.exp2(dot(keys, query_t_ref[:, cols]) * LOG2_SCALING)
            if diagonal:
                key = keys_at.start + lax.broadcasted_iota(jnp.int32, probs.shape, 0)
                column = cols.start + lax.broadcasted_iota(jnp.int32, probs.shape, 1)
                query = jnp.where(column < columns, 0, half) + lax.rem(column, half)
                probs = jnp.where(key <= query, probs, 0.0)
            grad_score = probs * dot(values, cotangent_t_ref[:, cols])
            grad_score = grad_score.astype(jnp.bfloat16)
            dv_ref[here, :] += dot(probs.astype(jnp.bfloat16), cotangent_ref[cols, :FEAT])
            dk_ref[here, :] += dot(grad_score, query_ref[cols, :FEAT])
            dq_ref[:, cols] += dot(kt_ref[key_block, :, keys_at], grad_score)

        def for_first_half(key_block, _):
            add_part(key_block, slice(0, BLOCK), slice(0, columns), False)
            return 0

        def for_both(key_block, _):
            add_part(key_block, slice(0, BLOCK), slice(0, 2 * columns), False)
            return 0

        lowest = start_of(block * BLOCK, first, second) // BLOCK
        lowest_of_both = start_of(block * BLOCK + half, first, second) // BLOCK
        lax.fori_loop(lowest, lowest_of_both, for_first_half, 0)
        lax.fori_loop(lowest_of_both, block, for_both, 0)
        add_part(block, slice(0, half), slice(0, 2 * columns), True)
        add_part(block, slice(half, BLOCK), slice(columns, 2 * columns), True)
        dq = (dq_ref[...] * SCALING).T.astype(jnp.bfloat16)
        for at, here, cols in places:
            grad_ref[here, cols] = dq[at]
        departure(block, query_cols, 0).start()
        return 0

    lax.fori_loop(0, blocks, one_query_block, 0)

    def finish(block, _):
        grad_ref[rows(block), key_cols] = (dk_ref[rows(block), :] * SCALING).astype(jnp.bfloat16)
        grad_ref[rows(block), value_cols] = dv_ref[rows(block), :].astype(jnp.bfloat16)
        departure(block, shared_cols, 1).start()
        return 0

    lax.fori_loop(0, blocks, finish, 0)
    for block in range(blocks):
        departure(block, query_cols, 0).wait()
        departure(block, shared_cols, 1).wait()


SMEM = pl.BlockSpec(memory_space=pltpu.SMEM)
VMEM = pl.BlockSpec(memory_space=pltpu.VMEM)
ANY = pl.BlockSpec(memory_space=pl.ANY)
SMALL = pltpu.CompilerParams(vmem_limit_bytes=32 * 2**20)
LARGE = pltpu.CompilerParams(vmem_limit_bytes=56 * 2**20)


def attend(group, doc_lengths, qkv, heads):
    tokens = qkv.shape[0]
    blocks = tokens // BLOCK
    columns = heads * BLOCK
    wide = jax.ShapeDtypeStruct((tokens, heads * FEAT), jnp.bfloat16)
    return pl.pallas_call(
        functools.partial(forward_kernel, heads),
        out_shape=(wide, wide),
        in_specs=[SMEM, SMEM, ANY],
        out_specs=(ANY, ANY),
        scratch_shapes=[
            pltpu.VMEM(qkv.shape, jnp.bfloat16),
            pltpu.VMEM(wide.shape, jnp.bfloat16),
            pltpu.VMEM(wide.shape, jnp.bfloat16),
            pltpu.VMEM((blocks, 2 * FEAT, BLOCK), jnp.bfloat16),
            pltpu.VMEM((columns, 2 * FEAT), jnp.bfloat16),
            pltpu.VMEM((blocks, columns, BLOCK), jnp.float32),
            pltpu.VMEM((columns, FEAT), jnp.float32),
            pltpu.VMEM((columns, FEAT), jnp.float32),
            pltpu.VMEM((columns, FEAT), jnp.float32),
            pltpu.SemaphoreType.DMA((blocks,)),
            pltpu.SemaphoreType.DMA((2, blocks)),
        ],
        compiler_params=LARGE,
        cost_estimate=pl.CostEstimate(
            flops=2 * 2 * heads * tokens * tokens * FEAT,
            bytes_accessed=4 * 2**20,
            transcendentals=heads * tokens * tokens // 2,
        ),
    )(group, doc_lengths, qkv)


def attend_back(group, doc_lengths, qkv, output, marks, cotangent, heads):
    tokens = qkv.shape[0]
    blocks = tokens // BLOCK
    columns = heads * BLOCK
    return pl.pallas_call(
        functools.partial(backward_kernel, heads),
        out_shape=jax.ShapeDtypeStruct(qkv.shape, jnp.bfloat16),
        in_specs=[SMEM, SMEM, ANY, ANY, ANY, ANY],
        out_specs=ANY,
        scratch_shapes=[
            pltpu.VMEM(qkv.shape, jnp.bfloat16),
            pltpu.VMEM(output.shape, jnp.bfloat16),
            pltpu.VMEM(marks.shape, jnp.bfloat16),
            pltpu.VMEM(cotangent.shape, jnp.bfloat16),
            pltpu.VMEM(qkv.shape, jnp.bfloat16),
            pltpu.VMEM((tokens, FEAT), jnp.bfloat16),
            pltpu.VMEM((blocks, FEAT, BLOCK), jnp.bfloat16),
            pltpu.VMEM((columns, 2 * FEAT), jnp.bfloat16),
            pltpu.VMEM((columns, 2 * FEAT), jnp.bfloat16),
            pltpu.VMEM((2 * FEAT, columns), jnp.bfloat16),
            pltpu.VMEM((2 * FEAT, columns), jnp.bfloat16),
            pltpu.VMEM((FEAT, columns), jnp.float32),
            pltpu.VMEM((tokens, FEAT), jnp.float32),
            pltpu.VMEM((tokens, FEAT), jnp.float32),
            pltpu.SemaphoreType.DMA((4, blocks)),
            pltpu.SemaphoreType.DMA((2, blocks)),
        ],
        compiler_params=LARGE,
        cost_estimate=pl.CostEstimate(
            flops=5 * 2 * heads * tokens * tokens * FEAT,
            bytes_accessed=7 * 2**20,
            transcendentals=heads * tokens * tokens // 2,
        ),
    )(group, doc_lengths, qkv, output, marks, cotangent)


def prologue_kernel(
    repeats,
    q_hbm,
    k_hbm,
    v_hbm,
    cot_hbm,
    qkv_hbm,
    by_device_hbm,
    q_ref,
    k_ref,
    v_ref,
    cot_ref,
    qkv_ref,
    by_device_ref,
    in_sems,
    out_sems,
):
    devices, tokens, width = by_device_hbm.shape
    parts = in_sems.shape[1]
    span = tokens // parts
    arrivals = [
        [
            pltpu.make_async_copy(
                source.at[part * span : (part + 1) * span, :],
                target.at[part * span : (part + 1) * span, :],
                in_sems.at[n, part],
            )
            for part in range(parts)
        ]
        for n, (source, target) in enumerate(
            ((q_hbm, q_ref), (k_hbm, k_ref), (v_hbm, v_ref), (cot_hbm, cot_ref))
        )
    ]
    for group in arrivals:
        for arrival in group:
            arrival.start()
    for group in arrivals[:3]:
        for arrival in group:
            arrival.wait()
    departures = []
    for device in range(devices):
        shared = slice(device // repeats * FEAT, (device // repeats + 1) * FEAT)
        qkv_ref[device, :, :width] = q_ref[:, device * width : (device + 1) * width]
        qkv_ref[device, :, width : width + FEAT] = k_ref[:, shared]
        qkv_ref[device, :, width + FEAT :] = v_ref[:, shared]
        departures.append(
            pltpu.make_async_copy(qkv_ref.at[device], qkv_hbm.at[device], out_sems.at[0, device])
        )
        departures[-1].start()
    for arrival in arrivals[3]:
        arrival.wait()
    for device in range(devices):
        by_device_ref[device] = cot_ref[:, device * width : (device + 1) * width]
        departures.append(
            pltpu.make_async_copy(
                by_device_ref.at[device], by_device_hbm.at[device], out_sems.at[1, device]
            )
        )
        departures[-1].start()
    for departure in departures:
        departure.wait()


def by_device(queries, key_vectors, value_vectors, grad_out, devices):
    tokens = queries.shape[0]
    width = queries.shape[1] // devices
    outs = (
        jax.ShapeDtypeStruct((devices, tokens, width + 2 * FEAT), jnp.bfloat16),
        jax.ShapeDtypeStruct((devices, tokens, width), jnp.bfloat16),
    )
    arrays = (queries, key_vectors, value_vectors, grad_out, *outs)
    return pl.pallas_call(
        functools.partial(prologue_kernel, devices // KV_HEADS),
        out_shape=outs,
        in_specs=[ANY] * 4,
        out_specs=(ANY, ANY),
        scratch_shapes=[pltpu.VMEM(array.shape, array.dtype) for array in arrays]
        + [pltpu.SemaphoreType.DMA((4, 4)), pltpu.SemaphoreType.DMA((2, devices))],
        compiler_params=LARGE,
    )(queries, key_vectors, value_vectors, grad_out)


def epilogue_kernel(repeats, grads_ref, attn_ref, out_ref, dq_ref, dk_ref, dv_ref):
    devices, _, width = attn_ref.shape
    for device in range(devices):
        cols = slice(device * width, (device + 1) * width)
        out_ref[:, cols] = attn_ref[device]
        dq_ref[:, cols] = grads_ref[device, :, :width]
    for head in range(devices // repeats):
        cols = slice(head * FEAT, (head + 1) * FEAT)
        for ref, at in ((dk_ref, width), (dv_ref, width + FEAT)):
            parts = [
                grads_ref[head * repeats + part, :, at : at + FEAT].astype(jnp.float32)
                for part in range(repeats)
            ]
            ref[:, cols] = functools.reduce(jnp.add, parts).astype(jnp.bfloat16)


def by_token(grads, attn):
    devices, tokens, width = attn.shape
    wide = jax.ShapeDtypeStruct((tokens, devices * width), jnp.bfloat16)
    narrow = jax.ShapeDtypeStruct((tokens, KV_HEADS * FEAT), jnp.bfloat16)
    return pl.pallas_call(
        functools.partial(epilogue_kernel, devices // KV_HEADS),
        out_shape=(wide, wide, narrow, narrow),
        in_specs=[VMEM] * 2,
        out_specs=(VMEM,) * 4,
        compiler_params=SMALL,
    )(grads, attn)


def over_heads(block):
    return lax.all_to_all(block, "head", split_axis=0, concat_axis=0, tiled=True)


def hop(block, distance):
    count = lax.axis_size("grp")
    return lax.ppermute(block, "grp", [(i, (i + distance) % count) for i in range(count)])


LONG_WAY = {5: 4, 6: 5}


def along_rows(block, distance, split=False):
    count = lax.axis_size("grp")
    distance %= count
    short = distance if 2 * distance <= count else distance - count
    parts = LONG_WAY.get(abs(short), 0) * block.shape[0] // 16
    if not parts or not split:
        return hop(block, short)
    long = short - count if short > 0 else short + count
    far = hop(block[:parts], long // 2)
    near = hop(block[parts:], short)
    far = hop(far, long - long // 2)
    return jnp.concatenate([far, near], axis=0)


def first_part(shift, cotangent):
    return along_rows(cotangent, -shift)


def last_part(shift, attn):
    return along_rows(attn, shift, split=True)


def shards(queries, key_vectors, value_vectors, grad_out, doc_lengths, parcel_shift):
    group = lax.axis_index("grp").astype(jnp.int32).reshape(1)
    doc_lengths = doc_lengths.T
    devices = lax.axis_size("head")
    heads = HEADS // devices
    shifts = range(1, lax.axis_size("grp"))
    choice = parcel_shift[0] - 1

    qkv, cotangent = by_device(queries, key_vectors, value_vectors, grad_out, devices)
    shape = cotangent.shape
    qkv = over_heads(qkv)
    cotangent = lax.switch(choice, [functools.partial(first_part, s) for s in shifts], cotangent)
    qkv, cotangent = lax.optimization_barrier((qkv, cotangent))
    qkv = qkv.reshape(shape[0] * shape[1], -1)
    cotangent = over_heads(cotangent)
    output, marks = attend(group, doc_lengths, qkv, heads)
    attn, cotangent = lax.optimization_barrier((output.reshape(shape), cotangent))
    attn = over_heads(attn)
    cotangent = cotangent.reshape(output.shape)
    grads = attend_back(group, doc_lengths, qkv, output, marks, cotangent, heads)
    grads = grads.reshape(shape[0], shape[1], -1)
    grads, attn = lax.optimization_barrier((grads, attn))
    grads = over_heads(grads)
    attn = lax.switch(choice, [functools.partial(last_part, s) for s in shifts], attn)
    return by_token(grads, attn)


def solution(mesh):
    split = P(("grp", "head"), None)
    return jax.shard_map(
        shards,
        mesh=mesh,
        in_specs=(split, split, split, split, P(), P()),
        out_specs=(split, split, split, split),
        check_vma=False,
    )
```
